128 devices in a mesh: dp: 16 (over y, x), owner: 8 (over z, core).
Axes of the slice: x: 4, y: 4, z: 4, core: 2. Of those that a mesh axis runs over, the one named last changes fastest.
Arguments:
- grad_part: bfloat16 [16, 16, 64, 12288], P('dp', None, 'owner'), may hold values from -0.29882812 to 0.29882812
- block_slot: int32 [12], replicated, may hold values from 0 to 23, as said below
- left_factor: float32 [24, 1024, 1024], P('owner', 'dp'), may hold values from -6 to 6
- right_factor: float32 [24, 1024, 1024], P('owner', 'dp'), may hold values from -6 to 6
- first_moment: bfloat16 [24, 1024, 1024], P('owner', 'dp'), may hold values from -0.59765625 to 0.59765625
- second_moment: bfloat16 [24, 1024, 1024], P('owner', 'dp'), may hold values from 0.0009994507 to 0.029907227
- left_basis: bfloat16 [24, 1024, 1024], P('owner'), may hold values from -0.1875 to 0.1875
- right_basis: bfloat16 [24, 1024, 1024], P('owner'), may hold values from -0.1875 to 0.1875
Outputs:
- new_left: float32 [24, 1024, 1024], P('owner', 'dp')
- new_right: float32 [24, 1024, 1024], P('owner', 'dp')
- new_first: bfloat16 [24, 1024, 1024], P('owner', 'dp')
- new_second: bfloat16 [24, 1024, 1024], P('owner', 'dp')
- update: bfloat16 [1024, 12288], P(('dp', 'owner'))
The draws below stay inside these ranges and needn't reach their ends.
Inputs may be any that keep to these rules, and one draw needn't show every extreme that they name: `block_slot`: the numbers are distinct; slot q belongs to owner q // 3; in every draw one owner holds 3 blocks.
All inputs are finite; a program needn't handle non-finite values.
Results may differ from the reference program's by a relative error of at most 0.02.
Values may be sent and summed in bfloat16 or wider, within the bound.
No kernel may reach another device: no remote copies, remote signals or barrier semaphores. Data moves between devices by JAX's collectives and lax.ppermute only.
A program may use at most 128 MiB of HBM per device.

```python
import math
import jax
import jax.numpy as jnp
from jax import lax

BS = 1024
SLOTS = 3
BLOCKS = 12
WIDTH = 12288
SLAB = 64
N_DP = 16
N_OWNER = 8


def draw_block_slot(key, part):
    key = jax.random.fold_in(key, 7)
    total = N_OWNER * SLOTS
    key_busy, key_order, key_blocks = jax.random.split(key, 3)
    busiest = jax.random.randint(key_busy, (), 0, N_OWNER)
    shuffled = jax.random.permutation(key_order, total).astype(jnp.int32)
    column = shuffled // SLOTS
    places = jnp.arange(total, dtype=jnp.int32)
    scores = jnp.where(column == busiest, places - total, places)
    ranked = shuffled[jnp.argsort(scores)]
    chosen = ranked[:BLOCKS]
    return chosen[jax.random.permutation(key_blocks, BLOCKS)].astype(jnp.int32)


def steps_of(own_key, shape, cuts, least, top_value):
    loudness, own = 1.0, jax.random.fold_in(own_key, 6)
    for dim, blocks in cuts:
        steps = jnp.exp(jax.random.uniform(jax.random.fold_in(own, dim), (blocks,), jnp.float32, least / len(cuts), top_value / len(cuts)))
        loudness = loudness * jnp.repeat(steps, shape[dim] // blocks).reshape([-1 if axis == dim else 1 for axis in range(len(shape))])
    return loudness


def bell_draw(rng, shape, width, most, shards=(), held_as=jnp.bfloat16):
    array = jax.random.normal(rng, shape, jnp.float32) * width
    if len(shards) > 0:
        array = steps_of(rng, shape, shards, -0.22, 0.18) * array
    return jnp.clip(array, min=-most, max=most).astype(held_as)


def setup_inputs(seed: int = 0) -> dict:
    key_list = jax.random.split(jax.random.key(seed), 9)
    grad_part = bell_draw(key_list[0], (N_DP, N_DP, SLAB, WIDTH), 0.05, 0.29882812, ((0, 16), (2, 8)))
    block_slot = draw_block_slot(jax.random.fold_in(key_list[8], 71), 0)
    left_factor = bell_draw(key_list[2], (N_OWNER * SLOTS, BS, BS), 1.0, 6.0, ((0, 8), (1, 16)), jnp.float32)
    right_factor = bell_draw(key_list[3], (N_OWNER * SLOTS, BS, BS), 1.0, 6.0, ((0, 8), (1, 16)), jnp.float32)
    first_moment = bell_draw(key_list[4], (N_OWNER * SLOTS, BS, BS), 0.1, 0.59765625, ((0, 8), (1, 16)))
    second_moment = jnp.clip(jnp.exp(math.log(0.029907227) - 3.3986496 * jax.random.uniform(key_list[5], (N_OWNER * SLOTS, BS, BS), jnp.float32) ** steps_of(key_list[5], (N_OWNER * SLOTS, BS, BS), ((0, 8), (1, 16)), -0.2, 0.2)), 0.0009994507, 0.029907227).astype(jnp.bfloat16)
    left_basis = bell_draw(key_list[6], (N_OWNER * SLOTS, BS, BS), BS ** -0.5, 0.1875, ((0, 8),))
    right_basis = bell_draw(key_list[7], (N_OWNER * SLOTS, BS, BS), BS ** -0.5, 0.1875, ((0, 8),))
    return {"grad_part": grad_part, "block_slot": block_slot, "left_factor": left_factor, "right_factor": right_factor, "first_moment": first_moment, "second_moment": second_moment, "left_basis": left_basis, "right_basis": right_basis}


BETA_FIRST = 0.9
BETA_SECOND = 0.95
BETA_FACTOR = 0.95
EPSILON = 1e-08

def reference(grad_part, block_slot, left_factor, right_factor, first_moment, second_moment, left_basis, right_basis):
    summed = lax.optimization_barrier(jnp.sum(grad_part.astype(jnp.float32), axis=0))
    gradient = summed.reshape(BS, WIDTH).astype(jnp.bfloat16)
    blockwise = jnp.transpose(gradient.reshape(BS, BLOCKS, BS), (1, 0, 2))

    def per_block(inputs):
        grad_block, position = inputs
        old_left = left_factor[position]
        old_right = right_factor[position]
        old_first = first_moment[position]
        old_second = second_moment[position]
        basis_left = left_basis[position]
        basis_right = right_basis[position]
        gram_left = jnp.dot(grad_block, grad_block.T, preferred_element_type=jnp.float32)
        gram_right = jnp.dot(grad_block.T, grad_block, preferred_element_type=jnp.float32)
        left_out = BETA_FACTOR * old_left + (1.0 - BETA_FACTOR) * gram_left
        right_out = BETA_FACTOR * old_right + (1.0 - BETA_FACTOR) * gram_right
        moment = (BETA_FIRST * old_first.astype(jnp.float32) + (1.0 - BETA_FIRST) * grad_block.astype(jnp.float32)).astype(jnp.bfloat16)
        half_grad = jnp.dot(basis_left.T, grad_block, preferred_element_type=jnp.float32).astype(jnp.bfloat16)
        rot_grad = jnp.dot(half_grad, basis_right, preferred_element_type=jnp.float32)
        half_mom = jnp.dot(basis_left.T, moment, preferred_element_type=jnp.float32).astype(jnp.bfloat16)
        rot_mom = jnp.dot(half_mom, basis_right, preferred_element_type=jnp.float32)
        variance = BETA_SECOND * old_second.astype(jnp.float32) + (1.0 - BETA_SECOND) * rot_grad * rot_grad
        direction = (rot_mom / (jnp.sqrt(variance) + EPSILON)).astype(jnp.bfloat16)
        back_half = jnp.dot(direction, basis_right.T, preferred_element_type=jnp.float32).astype(jnp.bfloat16)
        step_block = jnp.dot(basis_left, back_half, preferred_element_type=jnp.float32).astype(jnp.bfloat16)
        return (left_out, right_out, moment, variance.astype(jnp.bfloat16), step_block)
    lefts, rights, firsts, seconds, steps_all = lax.map(per_block, (blockwise, block_slot))
    total_slots = N_OWNER * SLOTS
    new_left = jnp.zeros((total_slots, BS, BS), jnp.float32).at[block_slot].set(lefts)
    new_right = jnp.zeros((total_slots, BS, BS), jnp.float32).at[block_slot].set(rights)
    new_first = jnp.zeros((total_slots, BS, BS), jnp.bfloat16).at[block_slot].set(firsts)
    new_second = jnp.zeros((total_slots, BS, BS), jnp.bfloat16).at[block_slot].set(seconds)
    update = jnp.transpose(steps_all, (1, 0, 2)).reshape(BS, WIDTH)
    return (new_left, new_right, new_first, new_second, update)
```

```python
import jax
import jax.numpy as jnp
from jax import lax
from jax.experimental import pallas as pl
from jax.experimental.pallas import tpu as pltpu
from jax.sharding import PartitionSpec as P

BETA_FIRST = 0.9
BETA_SECOND = 0.95
BETA_FACTOR = 0.95
EPSILON = 1e-08
F32 = jnp.float32
BF16 = jnp.bfloat16
HALF = 64
LANES = 128
VMEM_BYTES = 40 * 1024 * 1024

NN = (((1,), (0,)), ((), ()))
NT = (((1,), (1,)), ((), ()))
TN = (((0,), (0,)), ((), ()))


def dot(a, b, dims):
    return lax.dot_general(a, b, dims, preferred_element_type=F32)


def swap_halves(x):
    return pltpu.roll(x, HALF, 1)


def rotate_right_kernel(used_ref, grad_ref, moment_ref, second_ref, basis_ref, first_ref, packed_ref):
    slot = pl.program_id(0)
    used = used_ref[slot] > 0
    low = lax.broadcasted_iota(jnp.int32, (HALF, LANES), 1) < HALF
    grad = grad_ref[0]
    moment = (
        BETA_FIRST * moment_ref[0].astype(F32) + (1.0 - BETA_FIRST) * grad.astype(F32)
    ).astype(BF16)
    first_ref[0] = jnp.where(used, moment.astype(F32), 0.0).astype(BF16)
    both = jnp.concatenate([grad, moment], axis=0)
    turned = dot(both, basis_ref[0], NN)
    second = second_ref[0].astype(F32)
    for pair in range(packed_ref.shape[0] // 2):
        lanes = slice(pair * LANES, (pair + 1) * LANES)
        a = turned[:HALF, lanes]
        b = turned[HALF:, lanes]
        v = second[:, lanes]
        packed_ref[2 * pair, 0, :, :LANES] = jnp.where(low, a, swap_halves(b)).astype(BF16)
        packed_ref[2 * pair + 1, 0, :, :LANES] = jnp.where(low, swap_halves(a), b).astype(BF16)
        packed_ref[2 * pair, 0, :, LANES:] = v.astype(BF16)
        packed_ref[2 * pair + 1, 0, :, LANES:] = swap_halves(v).astype(BF16)


def rotate_left_kernel(packed_ref, basis_ref, out_ref):
    parts = packed_ref.shape[0]
    packed = packed_ref[...].reshape(parts * HALF, 2 * LANES)
    basis = basis_ref[0]
    turned = dot(packed[:, :LANES], basis, TN)
    second = packed[:, LANES:].astype(F32).T[:HALF]
    rot_grad = turned[:HALF]
    rot_mom = turned[HALF:]
    variance = BETA_SECOND * second + (1.0 - BETA_SECOND) * rot_grad * rot_grad
    direction = (rot_mom / (jnp.sqrt(variance) + EPSILON)).astype(BF16)
    step = dot(direction, basis, NT)
    out = jnp.concatenate([step, variance], axis=0).T.astype(BF16)
    out_ref[...] = out.reshape(out_ref.shape)


def step_kernel(used_ref, packed_ref, basis_ref, second_ref, step_ref):
    used = used_ref[pl.program_id(0)] > 0
    low = lax.broadcasted_iota(jnp.int32, (HALF, LANES), 1) < HALF
    lefts = []
    seconds = []
    for pair in range(packed_ref.shape[0] // 2):
        a = packed_ref[2 * pair, 0].astype(F32)
        b = packed_ref[2 * pair + 1, 0].astype(F32)
        lefts.append(jnp.where(low, a, swap_halves(b)).astype(BF16))
        seconds.append(jnp.where(low, swap_halves(a), b))
    second_ref[0] = jnp.where(used, jnp.concatenate(seconds, axis=1), 0.0).astype(BF16)
    left = jnp.concatenate(lefts, axis=1)
    step_ref[0] = dot(left, basis_ref[0], NT).astype(BF16)


def gram_kernel(used_ref, place_ref, whole_ref, rows_ref, left_ref, right_ref, new_left_ref, new_right_ref):
    used = used_ref[pl.program_id(0)] > 0
    place = place_ref[0]
    whole = whole_ref[...].reshape(left_ref.shape[2], left_ref.shape[2])
    gram_left = dot(rows_ref[0], whole, NT)
    start = pl.multiple_of((place // 2) * LANES, LANES)
    columns = whole_ref[:, 0, :, pl.ds(start, LANES)].reshape(left_ref.shape[2], LANES)
    gram_pair = dot(columns, whole, TN)
    gram_right = jnp.where(place % 2 == 0, gram_pair[:HALF], gram_pair[HALF:])
    new_left_ref[0] = jnp.where(
        used, BETA_FACTOR * left_ref[0] + (1.0 - BETA_FACTOR) * gram_left, 0.0
    )
    new_right_ref[0] = jnp.where(
        used, BETA_FACTOR * right_ref[0] + (1.0 - BETA_FACTOR) * gram_right, 0.0
    )


def on_device(
    grad_part,
    block_slot,
    left_factor,
    right_factor,
    first_moment,
    second_moment,
    left_basis,
    right_basis,
):
    owners = lax.axis_size("owner")
    replicas = lax.axis_size("dp")
    mine_dp = lax.axis_index("dp")
    mine_owner = lax.axis_index("owner")
    slots, slab, order = left_factor.shape
    part_rows = grad_part.shape[2]
    width = grad_part.shape[3]
    blocks = width // order

    slot_ids = jnp.arange(owners * slots, dtype=jnp.int32)
    matches = block_slot[None, :] == slot_ids[:, None]
    filled = jnp.any(matches, axis=1).astype(jnp.int32)
    holder = jnp.sum(jnp.where(matches, jnp.arange(blocks, dtype=jnp.int32)[None, :], 0), axis=1)
    used = lax.dynamic_slice_in_dim(filled, mine_owner * slots, slots)
    place = mine_dp.astype(jnp.int32).reshape(1)

    partials = lax.all_to_all(grad_part[0], "dp", split_axis=0, concat_axis=0, tiled=True)
    flat = jnp.sum(partials.astype(F32), axis=0).astype(BF16)
    by_block = flat.reshape(part_rows, blocks, order).transpose(1, 0, 2)
    outgoing = jnp.take(by_block, holder, axis=0).reshape(owners, slots, part_rows, order)
    incoming = lax.all_to_all(outgoing, "owner", split_axis=0, concat_axis=0, tiled=True)
    rows = incoming.transpose(1, 0, 2, 3).reshape(slots, slab, order)

    whole = lax.all_gather(rows, "dp", axis=0)

    smem = pl.BlockSpec(memory_space=pltpu.SMEM)
    slab_spec = pl.BlockSpec((1, slab, order), lambda q: (q, 0, 0))
    basis_spec = pl.BlockSpec((1, order, order), lambda q: (q, 0, 0))

    def chunk_spec(lanes):
        return pl.BlockSpec((replicas, 1, slab, lanes), lambda q: (0, q, 0, 0))

    def params():
        return pltpu.CompilerParams(vmem_limit_bytes=VMEM_BYTES)

    def cost(products, moved):
        return pl.CostEstimate(
            flops=2 * slots * products * slab * order * order, bytes_accessed=moved, transcendentals=0
        )

    slab_bf16 = jax.ShapeDtypeStruct((slots, slab, order), BF16)
    slab_f32 = jax.ShapeDtypeStruct((slots, slab, order), F32)
    new_first, packed = pl.pallas_call(
        rotate_right_kernel,
        grid=(slots,),
        in_specs=[smem, slab_spec, slab_spec, slab_spec, basis_spec],
        out_specs=[slab_spec, chunk_spec(2 * LANES)],
        out_shape=[slab_bf16, jax.ShapeDtypeStruct((replicas, slots, slab, 2 * LANES), BF16)],
        compiler_params=params(),
        cost_estimate=cost(2, 10 * 2**20),
        name="rotate_right",
    )(used, rows, first_moment, second_moment, right_basis)

    packed = lax.all_to_all(packed, "dp", split_axis=0, concat_axis=0, tiled=True)

    turned = pl.pallas_call(
        rotate_left_kernel,
        grid=(slots,),
        in_specs=[chunk_spec(2 * LANES), basis_spec],
        out_specs=chunk_spec(LANES),
        out_shape=jax.ShapeDtypeStruct((replicas, slots, slab, LANES), BF16),
        compiler_params=params(),
        cost_estimate=cost(3, 10 * 2**20),
        name="rotate_left",
    )(packed, left_basis)

    turned = lax.all_to_all(turned, "dp", split_axis=0, concat_axis=0, tiled=True)

    new_second, step = pl.pallas_call(
        step_kernel,
        grid=(slots,),
        in_specs=[smem, chunk_spec(LANES), basis_spec],
        out_specs=[slab_spec, slab_spec],
        out_shape=[slab_bf16, slab_bf16],
        compiler_params=params(),
        cost_estimate=cost(1, 8 * 2**20),
        name="step_rows",
    )(used, turned, right_basis)

    step = step.reshape(slots, owners, part_rows, order).transpose(1, 0, 2, 3)
    returned = lax.all_to_all(step, "owner", split_axis=0, concat_axis=0, tiled=True)
    picked = jnp.take(returned.reshape(owners * slots, part_rows, order), block_slot, axis=0)
    update = picked.transpose(1, 0, 2).reshape(part_rows, width)

    new_left, new_right = pl.pallas_call(
        gram_kernel,
        grid=(slots,),
        in_specs=[smem, smem, chunk_spec(order), slab_spec, slab_spec, slab_spec],
        out_specs=[slab_spec, slab_spec],
        out_shape=[slab_f32, slab_f32],
        compiler_params=params(),
        cost_estimate=cost(3, 10 * 2**20),
        name="factor_rows",
    )(used, place, whole, rows, left_factor, right_factor)

    return new_left, new_right, new_first, new_second, update


def solution(mesh):
    slabs = P("owner", "dp", None)
    whole_slots = P("owner", None, None)
    return jax.shard_map(
        on_device,
        mesh=mesh,
        in_specs=(
            P("dp", None, "owner", None),
            P(),
            slabs,
            slabs,
            slabs,
            slabs,
            whole_slots,
            whole_slots,
        ),
        out_specs=(slabs, slabs, slabs, slabs, P(("dp", "owner"), None)),
        check_vma=False,
    )
```

```python
import jax
import jax.numpy as jnp
from jax import lax
from jax.experimental import pallas as pl
from jax.experimental.pallas import tpu as pltpu
from jax.sharding import PartitionSpec as P

BETA_FIRST = 0.9
BETA_SECOND = 0.95
BETA_FACTOR = 0.95
EPSILON = 1e-08
F32 = jnp.float32
BF16 = jnp.bfloat16
HALF = 64
LANES = 128
VMEM_BYTES = 32 * 1024 * 1024
SMEM, VMEM, HBM, ANY = pltpu.SMEM, pltpu.VMEM, pltpu.HBM, pl.ANY
SIDE = 4

NN = (((1,), (0,)), ((), ()))
NT = (((1,), (1,)), ((), ()))
TN = (((0,), (0,)), ((), ()))


def dot(a, b, dims):
    return lax.dot_general(a, b, dims, preferred_element_type=F32)


def swap_halves(x):
    return pltpu.roll(x, HALF, 1)


def low_lanes(rows):
    return lax.broadcasted_iota(jnp.int32, (rows, LANES), 1) < HALF


def turn(index, by):
    return lax.rem(index + by, SIDE)


def start_all(copies):
    for copy in copies:
        copy.start()
    return copies


def wait_all(copies):
    for copy in copies:
        copy.wait()


def add(*terms):
    total = terms[0].astype(F32)
    for term in terms[1:]:
        total = total + term.astype(F32)
    return total.astype(BF16)


def first_send_kernel(here, grad, a1, b1, a3, b3, a2, b2, sems):
    y, x = here[0], here[1]
    half = grad.shape[3] // 2
    copies = []
    for by, a_out, b_out in ((1, a1, b1), (3, a3, b3), (2, a2, b2)):
        for source, target in (
            (grad.at[:, turn(x, by), :, pl.ds(0, half)], a_out),
            (grad.at[turn(y, by), :, :, pl.ds(half, half)], b_out),
        ):
            copies.append(pltpu.make_async_copy(source, target, sems.at[len(copies)]))
    wait_all(start_all(copies))


def fetch(source, target, sems):
    return start_all(
        [
            pltpu.make_async_copy(source.at[slot], target.at[slot], sems.at[slot])
            for slot in range(source.shape[0])
        ]
    )


def second_send_kernel(here, grad, a1, b1, a3, b3, a2, b2, p0, p1, p2, p3, q0, q1, q2, q3, a0, b0, sems):
    y, x = here[0], here[1]
    half = grad.shape[3] // 2
    own = [
        pltpu.make_async_copy(grad.at[:, x, :, pl.ds(0, half)], a0, sems.at[0]),
        pltpu.make_async_copy(grad.at[y, :, :, pl.ds(half, half)], b0, sems.at[1]),
    ]
    wait_all(start_all(own))
    for by, (p_out, q_out) in enumerate(((p0, q0), (p1, q1), (p2, q2), (p3, q3))):
        to_y = turn(y, by)
        to_x = turn(x, by)
        p_out[...] = add(a0[to_y], a1[to_y], a3[to_y], a2[to_y])
        q_out[...] = add(b0[to_x], b1[to_x], b3[to_x], b2[to_x])


def outgoing_kernel(holder, p0, p1, p2, p3, q0, q1, q2, q3, out, flat):
    order = out.shape[2]
    half_blocks = p0.shape[1] // order
    for block in range(half_blocks):
        lanes = slice(block * order, (block + 1) * order)
        flat[block] = add(p0[:, lanes], p1[:, lanes], p2[:, lanes], p3[:, lanes])
        flat[block + half_blocks] = add(q0[:, lanes], q1[:, lanes], q2[:, lanes], q3[:, lanes])
    for slot in range(out.shape[0]):
        out[slot] = flat[holder[slot]]


def moment_right_kernel(moment_hbm, second_hbm, basis_hbm, packed, moment, second, basis, small_sems, sems):
    small = start_all(
        [
            pltpu.make_async_copy(moment_hbm, moment, small_sems.at[0]),
            pltpu.make_async_copy(second_hbm, second, small_sems.at[1]),
        ]
    )
    arrivals = fetch(basis_hbm, basis, sems)
    wait_all(small)
    low = low_lanes(HALF)
    for slot in range(moment.shape[0]):
        arrivals[slot].wait()
        turned = dot(moment[slot], basis[slot], NN)
        for pair in range(packed.shape[0] // 2):
            lanes = slice(pair * LANES, (pair + 1) * LANES)
            a = turned[:, lanes]
            b = second[slot, :, lanes].astype(F32)
            packed[2 * pair, slot] = jnp.where(low, a, swap_halves(b)).astype(BF16)
            packed[2 * pair + 1, slot] = jnp.where(low, swap_halves(a), b).astype(BF16)


def moment_left_kernel(packed, basis_hbm, out, basis, sems):
    arrivals = fetch(basis_hbm, basis, sems)
    order = basis.shape[1]
    for slot in range(out.shape[0]):
        both = packed[:, slot].reshape(order, LANES)
        out[slot, HALF:] = both.astype(F32).T[HALF:]
        arrivals[slot].wait()
        out[slot, :HALF] = dot(both[:, :HALF], basis[slot], TN)


def rotate_right_kernel(used, rows, moment_hbm, basis_hbm, first, packed, moment, basis, small_sems, sems):
    small = pltpu.make_async_copy(moment_hbm, moment, small_sems.at[0])
    arrivals = fetch(basis_hbm, basis, sems)
    small.start()
    small.wait()
    half = HALF // 2
    low = low_lanes(half)
    for slot in range(rows.shape[0]):
        grad = rows[slot]
        mixed = BETA_FIRST * moment[slot].astype(F32) + (1.0 - BETA_FIRST) * grad.astype(F32)
        first[slot] = jnp.where(used[slot] > 0, mixed, 0.0).astype(BF16)
    for slot in range(rows.shape[0]):
        arrivals[slot].wait()
        turned = dot(rows[slot], basis[slot], NN)
        for pair in range(packed.shape[0] // 2):
            lanes = slice(pair * LANES, (pair + 1) * LANES)
            a = turned[:half, lanes]
            b = turned[half:, lanes]
            packed[2 * pair, slot] = jnp.where(low, a, swap_halves(b)).astype(BF16)
            packed[2 * pair + 1, slot] = jnp.where(low, swap_halves(a), b).astype(BF16)


def rotate_left_kernel(packed, basis_hbm, ready, out, basis, sems):
    arrivals = fetch(basis_hbm, basis, sems)
    order = basis.shape[1]
    parts, half = packed.shape[0], packed.shape[2]
    for slot in range(out.shape[1]):
        both = packed[:, slot].reshape(parts * half, LANES)
        arrivals[slot].wait()
        cut = basis[slot].reshape(parts, 2, half, order)
        rot_grad = dot(both[:, :HALF], cut[:, 0].reshape(parts * half, order), TN) + dot(
            both[:, HALF:], cut[:, 1].reshape(parts * half, order), TN
        )
        rot_mom = BETA_FIRST * ready[slot, :HALF] + (1.0 - BETA_FIRST) * rot_grad
        variance = BETA_SECOND * ready[slot, HALF:] + (1.0 - BETA_SECOND) * rot_grad * rot_grad
        direction = (rot_mom / (jnp.sqrt(variance) + EPSILON)).astype(BF16)
        step = dot(direction, basis[slot], NT)
        joined = jnp.concatenate([step, variance], axis=0).T.astype(BF16)
        out[:, slot] = joined.reshape(parts, HALF, LANES)


def step_kernel(used, packed, basis_hbm, second, step, basis, sems):
    arrivals = fetch(basis_hbm, basis, sems)
    low = low_lanes(HALF)
    for slot in range(second.shape[0]):
        lefts = []
        for pair in range(packed.shape[0] // 2):
            lanes = slice(pair * LANES, (pair + 1) * LANES)
            a = packed[2 * pair, slot].astype(F32)
            b = packed[2 * pair + 1, slot].astype(F32)
            lefts.append(jnp.where(low, a, swap_halves(b)).astype(BF16))
            v = jnp.where(low, swap_halves(a), b)
            second[slot, :, lanes] = jnp.where(used[slot] > 0, v, 0.0).astype(BF16)
        arrivals[slot].wait()
        moved = dot(jnp.concatenate(lefts, axis=1), basis[slot], NT)
        step[:, slot] = moved.reshape(step.shape[0], step.shape[2], step.shape[3]).astype(BF16)


def gram_tiles_kernel(
    here, rows, x1, y1, x3, y3, x2, y2,
    left0, left1, left2, left3, right0, right1, right2, right3,
    across, down, grams, sems,
):
    y, x = here[0], here[1]
    slots, slab, order = rows.shape
    lines = SIDE * slab
    start = pl.multiple_of(y * lines, lines)
    copies = []
    for back, (ref_x, ref_y) in enumerate(((rows, rows), (x1, y1), (x2, y2), (x3, y3))):
        copies.append(pltpu.make_async_copy(ref_x, across.at[turn(x, SIDE - back)], sems.at[0, back]))
        copies.append(pltpu.make_async_copy(ref_y, down.at[back], sems.at[1, back]))
    wait_all(start_all(copies))
    for slot in range(slots):
        panel = down[:, slot].reshape(lines, order)
        tile = dot(panel, across[:, slot].reshape(lines, order), NT)
        for back, out in enumerate((left0, left1, left2, left3)):
            out[slot] = tile[back * slab : (back + 1) * slab].astype(out.dtype)
        columns = down[:, slot, :, pl.ds(start, lines)].reshape(lines, lines)
        grams[...] = dot(columns, panel, TN).reshape(grams.shape)
        for by, out in enumerate((right0, right1, right2, right3)):
            out[slot] = grams[turn(x, by)].astype(out.dtype)


def gram_sum_kernel(
    here, used, left0, left1, left2, left3, right0, right1, right2, right3, left_hbm, right_hbm,
    new_left, new_right, left, right, sems,
):
    y = here[0]
    old = start_all(
        [pltpu.make_async_copy(left_hbm, left, sems.at[0]), pltpu.make_async_copy(right_hbm, right, sems.at[1])]
    )
    wait_all(old)
    lines = left0.shape[2]
    for slot in range(left.shape[0]):
        is_used = used[slot] > 0
        for ahead, tile in enumerate((left0, left1, left2, left3)):
            lanes = pl.ds(pl.multiple_of(turn(y, ahead) * lines, lines), lines)
            new_left[slot, :, lanes] = jnp.where(
                is_used, BETA_FACTOR * left[slot, :, lanes] + (1.0 - BETA_FACTOR) * tile[slot].astype(F32), 0.0
            )
        gram = right0[slot] + right1[slot].astype(F32) + right2[slot].astype(F32) + right3[slot].astype(F32)
        new_right[slot] = jnp.where(is_used, BETA_FACTOR * right[slot] + (1.0 - BETA_FACTOR) * gram, 0.0)


def along_x(value, by):
    pairs = [
        (y * SIDE + x, y * SIDE + (x + by) % SIDE) for y in range(SIDE) for x in range(SIDE)
    ]
    return lax.ppermute(value, "dp", pairs)


def along_y(value, by):
    pairs = [
        (y * SIDE + x, ((y + by) % SIDE) * SIDE + x) for y in range(SIDE) for x in range(SIDE)
    ]
    return lax.ppermute(value, "dp", pairs)


def call(kernel, name, ins, outs, scratch, products, moved):
    arrays = [pltpu.with_memory_space_constraint(array, space) if space == HBM else array for array, space in ins]
    return pl.pallas_call(
        kernel,
        in_specs=[pl.BlockSpec(memory_space=space) for _, space in ins],
        out_specs=[pl.BlockSpec(memory_space=space or VMEM) for _, _, space in outs],
        out_shape=[
            space(shape, dtype) if space == VMEM else jax.ShapeDtypeStruct(shape, dtype) for shape, dtype, space in outs
        ],
        scratch_shapes=scratch,
        compiler_params=pltpu.CompilerParams(vmem_limit_bytes=VMEM_BYTES),
        cost_estimate=pl.CostEstimate(flops=products * 2**27, bytes_accessed=moved * 2**20, transcendentals=0),
        name=name,
    )(*arrays)


def sum_replicas(grad, here, holder, slot_total, order, beside, between):
    rows, width = grad.shape[1], grad.shape[2]
    half = width // 2
    grad = grad.reshape(SIDE, SIDE, rows, width)
    line = (SIDE, rows, half)
    sent = call(
        first_send_kernel, "first_send", [(here, SMEM), (grad, HBM)], [(line, BF16, VMEM)] * 6,
        [pltpu.SemaphoreType.DMA((6,))], 0, 5,
    )
    got = []
    for k, by in enumerate((1, 3, 2)):
        got += [along_x(sent[2 * k], by), along_y(sent[2 * k + 1], by)]
    got, early = lax.optimization_barrier((got, beside()))
    pieces = call(
        second_send_kernel, "second_send", [(here, SMEM), (grad, HBM)] + [(value, VMEM) for value in got],
        [((rows, half), BF16, None if by % SIDE == 0 else VMEM) for by in range(2 * SIDE)],
        [pltpu.VMEM(line, BF16), pltpu.VMEM(line, BF16), pltpu.SemaphoreType.DMA((2,))], 0, 4,
    )
    early = between(early)
    p, q = [pieces[0]], [pieces[4]]
    for by in (1, 3, 2):
        p.append(along_y(pieces[by], by))
        q.append(along_x(pieces[4 + by], by))
    p, q, early = lax.optimization_barrier((p, q, early))
    outgoing = call(
        outgoing_kernel, "outgoing", [(holder, SMEM)] + [(value, VMEM) for value in p + q],
        [((slot_total, rows, order), BF16, VMEM)], [pltpu.VMEM((width // order, rows, order), BF16)], 0, 1,
    )[0]
    return outgoing, early


def on_device(
    grad_part,
    block_slot,
    left_factor,
    right_factor,
    first_moment,
    second_moment,
    left_basis,
    right_basis,
):
    owners = lax.axis_size("owner")
    replicas = lax.axis_size("dp")
    mine_dp = lax.axis_index("dp").astype(jnp.int32)
    mine_owner = lax.axis_index("owner")
    slots, slab, order = left_factor.shape
    part_rows = grad_part.shape[2]
    width = grad_part.shape[3]
    blocks = width // order

    slot_ids = jnp.arange(owners * slots, dtype=jnp.int32)
    matches = block_slot[None, :] == slot_ids[:, None]
    filled = jnp.any(matches, axis=1).astype(jnp.int32)
    holder = jnp.sum(jnp.where(matches, jnp.arange(blocks, dtype=jnp.int32)[None, :], 0), axis=1)
    used = lax.dynamic_slice_in_dim(filled, mine_owner * slots, slots)
    here = jnp.stack([mine_dp // SIDE, mine_dp % SIDE])

    slabs = (slots, slab, order)

    def exchange(value, axis):
        return lax.all_to_all(value, axis, split_axis=0, concat_axis=0, tiled=True)

    basis_scratch = [pltpu.VMEM((slots, order, order), BF16), pltpu.SemaphoreType.DMA((slots,))]
    chunks = (replicas, slots, slab, LANES)

    def moment_right():
        return call(
            moment_right_kernel, "moment_right",
            [(first_moment, HBM), (second_moment, HBM), (right_basis, HBM)], [(chunks, BF16, VMEM)],
            [pltpu.VMEM(slabs, BF16), pltpu.VMEM(slabs, BF16), basis_scratch[0], pltpu.SemaphoreType.DMA((2,)), basis_scratch[1]],
            3, 8,
        )[0]

    outgoing, early = sum_replicas(
        grad_part[0], here, holder, owners * slots, order, moment_right, lambda value: exchange(value, "dp")
    )
    incoming = exchange(outgoing.reshape(owners, slots, part_rows, order), "owner")
    rows = incoming.transpose(1, 0, 2, 3).reshape(slabs)

    new_first, packed = call(
        rotate_right_kernel, "rotate_right",
        [(used, SMEM), (rows, VMEM), (first_moment, HBM), (right_basis, HBM)],
        [(slabs, BF16, None), ((replicas, slots, slab // 2, LANES), BF16, VMEM)],
        [pltpu.VMEM(slabs, BF16), basis_scratch[0], pltpu.SemaphoreType.DMA((1,)), basis_scratch[1]], 3, 8,
    )
    rows, packed, early = lax.optimization_barrier((rows, packed, early))
    packed = exchange(packed, "dp")
    near = []
    for by in (1, 3):
        near += [along_x(rows, by), along_y(rows, by)]
    near.append(along_x(rows, 2))
    ready = call(
        moment_left_kernel, "moment_left", [(early, VMEM), (left_basis, HBM)],
        [((slots, 2 * slab, order), F32, VMEM)], basis_scratch, 3, 8,
    )[0]
    rows, ready = lax.optimization_barrier((rows, ready))
    near.append(along_y(rows, 2))
    turned = call(
        rotate_left_kernel, "rotate_left", [(packed, VMEM), (left_basis, HBM), (ready, VMEM)],
        [(chunks, BF16, VMEM)], basis_scratch, 9, 8,
    )[0]
    near, turned = lax.optimization_barrier((near, turned))
    turned = exchange(turned, "dp")
    tiles = call(
        gram_tiles_kernel, "gram_tiles", [(here, SMEM)] + [(value, ANY) for value in [rows] + near],
        [((slots, slab, SIDE * slab), F32 if k == 0 else BF16, VMEM) for k in range(SIDE)]
        + [(slabs, F32 if k == 0 else BF16, VMEM) for k in range(SIDE)],
        [
            pltpu.VMEM((SIDE, slots, slab, order), BF16), pltpu.VMEM((SIDE, slots, slab, order), BF16),
            pltpu.VMEM((SIDE, slab, order), F32), pltpu.SemaphoreType.DMA((2, SIDE)),
        ],
        9, 6,
    )
    lefts = [tiles[0]] + [along_y(tiles[back], SIDE - back) for back in (1, 2, 3)]
    rights = [tiles[SIDE]] + [along_x(tiles[SIDE + by], by) for by in (1, 2, 3)]
    lefts, turned = lax.optimization_barrier((lefts, turned))
    new_second, step = call(
        step_kernel, "step_rows", [(used, SMEM), (turned, VMEM), (right_basis, HBM)],
        [(slabs, BF16, None), ((owners, slots, part_rows, order), BF16, VMEM)], basis_scratch, 3, 8,
    )
    returned = exchange(step, "owner")
    rights, step = lax.optimization_barrier((rights, step))
    new_left, new_right = call(
        gram_sum_kernel, "gram_sum",
        [(here, SMEM), (used, SMEM)] + [(value, VMEM) for value in lefts + rights]
        + [(left_factor, HBM), (right_factor, HBM)],
        [(slabs, F32, None)] * 2,
        [pltpu.VMEM(slabs, F32), pltpu.VMEM(slabs, F32), pltpu.SemaphoreType.DMA((2,))], 0, 8,
    )

    picked = returned.reshape(owners * slots, part_rows, order).at[block_slot].get(mode="promise_in_bounds")
    update = picked.transpose(1, 0, 2).reshape(part_rows, width)
    return new_left, new_right, new_first, new_second, update


def solution(mesh):
    slabs = P("owner", "dp", None)
    whole_slots = P("owner", None, None)
    return jax.shard_map(
        on_device,
        mesh=mesh,
        in_specs=(
            P("dp", None, "owner", None),
            P(),
            slabs,
            slabs,
            slabs,
            slabs,
            whole_slots,
            whole_slots,
        ),
        out_specs=(slabs, slabs, slabs, slabs, P(("dp", "owner"), None)),
        check_vma=False,
    )
```

```python
import jax
import jax.numpy as jnp
from jax import lax
from jax.experimental import pallas as pl
from jax.experimental.pallas import tpu as pltpu
from jax.sharding import PartitionSpec as P

BETA_FIRST = 0.9
BETA_SECOND = 0.95
BETA_FACTOR = 0.95
EPSILON = 1e-08
F32 = jnp.float32
BF16 = jnp.bfloat16
HALF = 64
LANES = 128
VMEM_BYTES = 32 * 1024 * 1024
SMEM, VMEM, HBM, ANY = pltpu.SMEM, pltpu.VMEM, pltpu.HBM, pl.ANY
SIDE = 4

NN = (((1,), (0,)), ((), ()))
NT = (((1,), (1,)), ((), ()))
TN = (((0,), (0,)), ((), ()))


def dot(a, b, dims):
    return lax.dot_general(a, b, dims, preferred_element_type=F32)


def swap_halves(x):
    return pltpu.roll(x, HALF, 1)


def low_lanes(rows):
    return lax.broadcasted_iota(jnp.int32, (rows, LANES), 1) < HALF


def turn(index, by):
    return lax.rem(index + by, SIDE)


def start_all(copies):
    for copy in copies:
        copy.start()
    return copies


def wait_all(copies):
    for copy in copies:
        copy.wait()


def add(*terms):
    total = terms[0].astype(F32)
    for term in terms[1:]:
        total = total + term.astype(F32)
    return total.astype(BF16)


def first_send_kernel(here, grad, a1, b1, a3, b3, a2, b2, sems):
    y, x = here[0], here[1]
    half = grad.shape[3] // 2
    copies = []
    for by, a_out, b_out in ((1, a1, b1), (3, a3, b3), (2, a2, b2)):
        for source, target in (
            (grad.at[:, turn(x, by), :, pl.ds(0, half)], a_out),
            (grad.at[turn(y, by), :, :, pl.ds(half, half)], b_out),
        ):
            copies.append(pltpu.make_async_copy(source, target, sems.at[len(copies)]))
    wait_all(start_all(copies))


def fetch(source, target, sems):
    return start_all(
        [
            pltpu.make_async_copy(source.at[slot], target.at[slot], sems.at[slot])
            for slot in range(source.shape[0])
        ]
    )


def second_send_kernel(here, grad, a1, b1, a3, b3, a2, b2, p0, p1, p2, p3, q0, q1, q2, q3, a0, b0, sems):
    y, x = here[0], here[1]
    half = grad.shape[3] // 2
    own = [
        pltpu.make_async_copy(grad.at[:, x, :, pl.ds(0, half)], a0, sems.at[0]),
        pltpu.make_async_copy(grad.at[y, :, :, pl.ds(half, half)], b0, sems.at[1]),
    ]
    wait_all(start_all(own))
    for by, (p_out, q_out) in enumerate(((p0, q0), (p1, q1), (p2, q2), (p3, q3))):
        to_y = turn(y, by)
        to_x = turn(x, by)
        p_out[...] = add(a0[to_y], a1[to_y], a3[to_y], a2[to_y])
        q_out[...] = add(b0[to_x], b1[to_x], b3[to_x], b2[to_x])


def outgoing_kernel(holder, p0, p1, p2, p3, q0, q1, q2, q3, out, flat):
    order = out.shape[2]
    half_blocks = p0.shape[1] // order
    for block in range(half_blocks):
        lanes = slice(block * order, (block + 1) * order)
        flat[block] = add(p0[:, lanes], p1[:, lanes], p2[:, lanes], p3[:, lanes])
        flat[block + half_blocks] = add(q0[:, lanes], q1[:, lanes], q2[:, lanes], q3[:, lanes])
    for slot in range(out.shape[0]):
        out[slot] = flat[holder[slot]]


def moment_right_kernel(moment_hbm, second_hbm, basis_hbm, packed, moment, second, basis, small_sems, sems):
    small = start_all(
        [
            pltpu.make_async_copy(moment_hbm, moment, small_sems.at[0]),
            pltpu.make_async_copy(second_hbm, second, small_sems.at[1]),
        ]
    )
    arrivals = fetch(basis_hbm, basis, sems)
    wait_all(small)
    low = low_lanes(HALF)
    for slot in range(moment.shape[0]):
        arrivals[slot].wait()
        turned = dot(moment[slot], basis[slot], NN)
        for pair in range(packed.shape[0] // 2):
            lanes = slice(pair * LANES, (pair + 1) * LANES)
            a = turned[:, lanes]
            b = second[slot, :, lanes].astype(F32)
            packed[2 * pair, slot] = jnp.where(low, a, swap_halves(b)).astype(BF16)
            packed[2 * pair + 1, slot] = jnp.where(low, swap_halves(a), b).astype(BF16)


def moment_left_kernel(packed, basis_hbm, out, basis, sems):
    arrivals = fetch(basis_hbm, basis, sems)
    order = basis.shape[1]
    for slot in range(out.shape[0]):
        both = packed[:, slot].reshape(order, LANES)
        out[slot, HALF:] = both.astype(F32).T[HALF:]
        arrivals[slot].wait()
        out[slot, :HALF] = dot(both[:, :HALF], basis[slot], TN)


def rotate_right_kernel(used, rows, moment_hbm, basis_hbm, first, packed, moment, basis, small_sems, sems):
    small = pltpu.make_async_copy(moment_hbm, moment, small_sems.at[0])
    arrivals = fetch(basis_hbm, basis, sems)
    small.start()
    small.wait()
    half = HALF // 2
    low = low_lanes(half)
    for slot in range(rows.shape[0]):
        grad = rows[slot]
        mixed = BETA_FIRST * moment[slot].astype(F32) + (1.0 - BETA_FIRST) * grad.astype(F32)
        first[slot] = jnp.where(used[slot] > 0, mixed, 0.0).astype(BF16)
    for slot in range(rows.shape[0]):
        arrivals[slot].wait()
        turned = dot(rows[slot], basis[slot], NN)
        for pair in range(packed.shape[0] // 2):
            lanes = slice(pair * LANES, (pair + 1) * LANES)
            a = turned[:half, lanes]
            b = turned[half:, lanes]
            packed[2 * pair, slot] = jnp.where(low, a, swap_halves(b)).astype(BF16)
            packed[2 * pair + 1, slot] = jnp.where(low, swap_halves(a), b).astype(BF16)


def rotate_left_kernel(packed, basis_hbm, ready, out, basis, sems):
    arrivals = fetch(basis_hbm, basis, sems)
    order = basis.shape[1]
    parts, half = packed.shape[0], packed.shape[2]
    for slot in range(out.shape[1]):
        both = packed[:, slot].reshape(parts * half, LANES)
        arrivals[slot].wait()
        cut = basis[slot].reshape(parts, 2, half, order)
        rot_grad = dot(both[:, :HALF], cut[:, 0].reshape(parts * half, order), TN) + dot(
            both[:, HALF:], cut[:, 1].reshape(parts * half, order), TN
        )
        rot_mom = BETA_FIRST * ready[slot, :HALF] + (1.0 - BETA_FIRST) * rot_grad
        variance = BETA_SECOND * ready[slot, HALF:] + (1.0 - BETA_SECOND) * rot_grad * rot_grad
        direction = (rot_mom / (jnp.sqrt(variance) + EPSILON)).astype(BF16)
        step = dot(direction, basis[slot], NT)
        joined = jnp.concatenate([step, variance], axis=0).T.astype(BF16)
        out[:, slot] = joined.reshape(parts, HALF, LANES)


def step_kernel(used, packed, basis_hbm, second, step, basis, sems):
    arrivals = fetch(basis_hbm, basis, sems)
    low = low_lanes(HALF)
    for slot in range(second.shape[0]):
        lefts = []
        for pair in range(packed.shape[0] // 2):
            lanes = slice(pair * LANES, (pair + 1) * LANES)
            a = packed[2 * pair, slot].astype(F32)
            b = packed[2 * pair + 1, slot].astype(F32)
            lefts.append(jnp.where(low, a, swap_halves(b)).astype(BF16))
            v = jnp.where(low, swap_halves(a), b)
            second[slot, :, lanes] = jnp.where(used[slot] > 0, v, 0.0).astype(BF16)
        arrivals[slot].wait()
        moved = dot(jnp.concatenate(lefts, axis=1), basis[slot], NT)
        step[:, slot] = moved.reshape(step.shape[0], step.shape[2], step.shape[3]).astype(BF16)


def gram_tiles_kernel(
    here, rows, x2, y2, x1, y1, y3,
    own, left0, left1, left2, left3, right0, right1, right2, right3,
    across, down, grams, sems,
):
    y, x = here[0], here[1]
    slots, slab, order = rows.shape
    lines = SIDE * slab
    start = pl.multiple_of(y * lines, lines)
    copies = []
    for back, ref in enumerate((x1, x2)):
        copies.append(pltpu.make_async_copy(ref, across.at[back], sems.at[0, back]))
    for back, ref in enumerate((rows, y1, y2, y3)):
        copies.append(pltpu.make_async_copy(ref, down.at[back], sems.at[1, back]))
    wait_all(start_all(copies))
    for slot in range(slots):
        panel = down[:, slot].reshape(lines, order)
        tile = dot(panel, across[:, slot].reshape(2 * slab, order), NT)
        own[slot] = dot(down[0, slot], panel, NT)
        for back, out in enumerate((left0, left1, left2, left3)):
            out[slot] = tile[back * slab : (back + 1) * slab].astype(out.dtype)
        columns = down[:, slot, :, pl.ds(start, lines)].reshape(lines, lines)
        grams[...] = dot(columns, panel, TN).reshape(grams.shape)
        for by, out in enumerate((right0, right1, right2, right3)):
            out[slot, :, :order] = grams[turn(x, by)].astype(out.dtype)
        right3[slot, :, order:] = dot(across[0, slot], panel, NT).astype(BF16)


def spread(pair, which):
    other = swap_halves(pair)
    low = low_lanes(pair.shape[0])
    twice = jnp.where(low, pair, other) if which == 0 else jnp.where(low, other, pair)
    return jnp.concatenate([twice, twice], axis=1)


def gram_sum_kernel(
    here, used, own, left0, left1, left2, left3, right0, right1, right2, right3, left_hbm, right_hbm,
    new_left, new_right, left, right, sems,
):
    y, x = here[0], here[1]
    old = start_all(
        [pltpu.make_async_copy(left_hbm, left, sems.at[0]), pltpu.make_async_copy(right_hbm, right, sems.at[1])]
    )
    slots, slab, order = left.shape
    lines = own.shape[2]
    column = lax.broadcasted_iota(jnp.int32, (slab, lines), 1) // HALF
    wait_all(old)
    for slot in range(slots):
        is_used = used[slot] > 0
        for ahead, tile in enumerate((left0, left1, left2, left3)):
            back = (SIDE - ahead) % SIDE
            same = spread(own[slot, :, back // 2 * LANES :][:, :LANES], back % 2)
            first = order + back // 2 * LANES
            ahead_x = spread(right3[slot, :, first : first + LANES].astype(F32), back % 2)
            tile = tile[slot].astype(F32)
            gram = jnp.where(column == turn(x, 1), ahead_x, same)
            gram = jnp.where(column == turn(x, 3), spread(tile, 0), gram)
            gram = jnp.where(column == turn(x, 2), spread(tile, 1), gram)
            lanes = pl.ds(pl.multiple_of(turn(y, ahead) * lines, lines), lines)
            new_left[slot, :, lanes] = jnp.where(
                is_used, BETA_FACTOR * left[slot, :, lanes] + (1.0 - BETA_FACTOR) * gram, 0.0
            )
        gram = right0[slot]
        for term in (right1, right2, right3):
            gram = gram + term[slot, :, :order].astype(F32)
        new_right[slot] = jnp.where(is_used, BETA_FACTOR * right[slot] + (1.0 - BETA_FACTOR) * gram, 0.0)


def along_x(value, by):
    pairs = [
        (y * SIDE + x, y * SIDE + (x + by) % SIDE) for y in range(SIDE) for x in range(SIDE)
    ]
    return lax.ppermute(value, "dp", pairs)


def along_y(value, by):
    pairs = [
        (y * SIDE + x, ((y + by) % SIDE) * SIDE + x) for y in range(SIDE) for x in range(SIDE)
    ]
    return lax.ppermute(value, "dp", pairs)


def call(kernel, name, ins, outs, scratch, products, moved):
    arrays = [pltpu.with_memory_space_constraint(array, space) if space == HBM else array for array, space in ins]
    return pl.pallas_call(
        kernel,
        in_specs=[pl.BlockSpec(memory_space=space) for _, space in ins],
        out_specs=[pl.BlockSpec(memory_space=space or VMEM) for _, _, space in outs],
        out_shape=[
            space(shape, dtype) if space == VMEM else jax.ShapeDtypeStruct(shape, dtype) for shape, dtype, space in outs
        ],
        scratch_shapes=scratch,
        compiler_params=pltpu.CompilerParams(vmem_limit_bytes=VMEM_BYTES),
        cost_estimate=pl.CostEstimate(flops=products * 2**27, bytes_accessed=moved * 2**20, transcendentals=0),
        name=name,
    )(*arrays)


def sum_replicas(grad, here, holder, slot_total, order, beside, between):
    rows, width = grad.shape[1], grad.shape[2]
    half = width // 2
    grad = grad.reshape(SIDE, SIDE, rows, width)
    line = (SIDE, rows, half)
    sent = call(
        first_send_kernel, "first_send", [(here, SMEM), (grad, HBM)], [(line, BF16, VMEM)] * 6,
        [pltpu.SemaphoreType.DMA((6,))], 0, 5,
    )
    got = []
    for k, by in enumerate((1, 3, 2)):
        got += [along_x(sent[2 * k], by), along_y(sent[2 * k + 1], by)]
    got, early = lax.optimization_barrier((got, beside()))
    early = between(early)
    pieces = call(
        second_send_kernel, "second_send", [(here, SMEM), (grad, HBM)] + [(value, VMEM) for value in got],
        [((rows, half), BF16, None if by % SIDE == 0 else VMEM) for by in range(2 * SIDE)],
        [pltpu.VMEM(line, BF16), pltpu.VMEM(line, BF16), pltpu.SemaphoreType.DMA((2,))], 0, 4,
    )
    p, q = [pieces[0]], [pieces[4]]
    for by in (1, 3, 2):
        p.append(along_y(pieces[by], by))
        q.append(along_x(pieces[4 + by], by))
    p, q, early = lax.optimization_barrier((p, q, early))
    outgoing = call(
        outgoing_kernel, "outgoing", [(holder, SMEM)] + [(value, VMEM) for value in p + q],
        [((slot_total, rows, order), BF16, VMEM)], [pltpu.VMEM((width // order, rows, order), BF16)], 0, 1,
    )[0]
    return outgoing, early


def on_device(
    grad_part,
    block_slot,
    left_factor,
    right_factor,
    first_moment,
    second_moment,
    left_basis,
    right_basis,
):
    owners = lax.axis_size("owner")
    replicas = lax.axis_size("dp")
    mine_dp = lax.axis_index("dp").astype(jnp.int32)
    mine_owner = lax.axis_index("owner")
    slots, slab, order = left_factor.shape
    part_rows = grad_part.shape[2]
    width = grad_part.shape[3]
    blocks = width // order

    slot_ids = jnp.arange(owners * slots, dtype=jnp.int32)
    matches = block_slot[None, :] == slot_ids[:, None]
    filled = jnp.any(matches, axis=1).astype(jnp.int32)
    holder = jnp.sum(jnp.where(matches, jnp.arange(blocks, dtype=jnp.int32)[None, :], 0), axis=1)
    used = lax.dynamic_slice_in_dim(filled, mine_owner * slots, slots)
    here = jnp.stack([mine_dp // SIDE, mine_dp % SIDE])

    slabs = (slots, slab, order)

    def exchange(value, axis):
        return lax.all_to_all(value, axis, split_axis=0, concat_axis=0, tiled=True)

    basis_scratch = [pltpu.VMEM((slots, order, order), BF16), pltpu.SemaphoreType.DMA((slots,))]
    chunks = (replicas, slots, slab, LANES)

    def moment_right():
        return call(
            moment_right_kernel, "moment_right",
            [(first_moment, HBM), (second_moment, HBM), (right_basis, HBM)], [(chunks, BF16, VMEM)],
            [pltpu.VMEM(slabs, BF16), pltpu.VMEM(slabs, BF16), basis_scratch[0], pltpu.SemaphoreType.DMA((2,)), basis_scratch[1]],
            3, 8,
        )[0]

    outgoing, early = sum_replicas(
        grad_part[0], here, holder, owners * slots, order, moment_right, lambda value: exchange(value, "dp")
    )
    incoming = exchange(outgoing.reshape(owners, slots, part_rows, order), "owner")
    ready = call(
        moment_left_kernel, "moment_left", [(early, VMEM), (left_basis, HBM)],
        [((slots, 2 * slab, order), F32, VMEM)], basis_scratch, 3, 8,
    )[0]
    incoming, ready = lax.optimization_barrier((incoming, ready))
    rows = incoming.transpose(1, 0, 2, 3).reshape(slabs)

    new_first, packed = call(
        rotate_right_kernel, "rotate_right",
        [(used, SMEM), (rows, VMEM), (first_moment, HBM), (right_basis, HBM)],
        [(slabs, BF16, None), ((replicas, slots, slab // 2, LANES), BF16, VMEM)],
        [pltpu.VMEM(slabs, BF16), basis_scratch[0], pltpu.SemaphoreType.DMA((1,)), basis_scratch[1]], 3, 8,
    )
    rows, packed = lax.optimization_barrier((rows, packed))
    packed = exchange(packed, "dp")
    near = []
    for by in (2, 1):
        near += [along_x(rows, by), along_y(rows, by)]
    near.append(along_y(rows, 3))
    turned = call(
        rotate_left_kernel, "rotate_left", [(packed, VMEM), (left_basis, HBM), (ready, VMEM)],
        [(chunks, BF16, VMEM)], basis_scratch, 9, 8,
    )[0]
    near, turned = lax.optimization_barrier((near, turned))
    turned = exchange(turned, "dp")
    tiles = call(
        gram_tiles_kernel, "gram_tiles", [(here, SMEM)] + [(value, HBM) for value in [rows] + near],
        [((slots, slab, SIDE * slab), F32, VMEM)]
        + [((slots, slab, 2 * slab), F32 if k == 0 else BF16, VMEM) for k in range(SIDE)]
        + [(slabs, F32, VMEM), (slabs, BF16, VMEM), (slabs, BF16, VMEM), ((slots, slab, order + SIDE * slab), BF16, VMEM)],
        [
            pltpu.VMEM((2, slots, slab, order), BF16), pltpu.VMEM((SIDE, slots, slab, order), BF16),
            pltpu.VMEM((SIDE, slab, order), F32), pltpu.SemaphoreType.DMA((2, SIDE)),
        ],
        9, 6,
    )
    lefts = [tiles[1]] + [along_y(tiles[1 + back], SIDE - back) for back in (1, 2, 3)]
    rights = [tiles[1 + SIDE]] + [along_x(tiles[1 + SIDE + by], by) for by in (1, 2, 3)]
    new_second, step = call(
        step_kernel, "step_rows", [(used, SMEM), (turned, VMEM), (right_basis, HBM)],
        [(slabs, BF16, None), ((owners, slots, part_rows, order), BF16, VMEM)], basis_scratch, 3, 8,
    )
    returned = exchange(step, "owner")
    rights, step = lax.optimization_barrier((rights, step))
    new_left, new_right = call(
        gram_sum_kernel, "gram_sum",
        [(here, SMEM), (used, SMEM)] + [(value, VMEM) for value in [tiles[0]] + lefts + rights]
        + [(left_factor, HBM), (right_factor, HBM)],
        [(slabs, F32, None)] * 2,
        [pltpu.VMEM(slabs, F32), pltpu.VMEM(slabs, F32), pltpu.SemaphoreType.DMA((2,))], 0, 8,
    )

    picked = returned.reshape(owners * slots, part_rows, order).at[block_slot].get(mode="promise_in_bounds")
    update = picked.transpose(1, 0, 2).reshape(part_rows, width)
    return new_left, new_right, new_first, new_second, update


def solution(mesh):
    slabs = P("owner", "dp", None)
    whole_slots = P("owner", None, None)
    return jax.shard_map(
        on_device,
        mesh=mesh,
        in_specs=(
            P("dp", None, "owner", None),
            P(),
            slabs,
            slabs,
            slabs,
            slabs,
            whole_slots,
            whole_slots,
        ),
        out_specs=(slabs, slabs, slabs, slabs, P(("dp", "owner"), None)),
        check_vma=False,
    )
```

```python
import functools

import jax
import jax.numpy as jnp
from jax import lax
from jax.experimental import pallas as pl
from jax.experimental.pallas import tpu as pltpu
from jax.sharding import PartitionSpec as P

BETA_FIRST = 0.9
BETA_SECOND = 0.95
BETA_FACTOR = 0.95
EPSILON = 1e-08
F32 = jnp.float32
BF16 = jnp.bfloat16
HALF = 64
LANES = 128
VMEM_BYTES = 32 * 1024 * 1024
SMEM, VMEM, HBM, ANY = pltpu.SMEM, pltpu.VMEM, pltpu.HBM, pl.ANY
SIDE = 4

NN = (((1,), (0,)), ((), ()))
NT = (((1,), (1,)), ((), ()))
TN = (((0,), (0,)), ((), ()))


def dot(a, b, dims):
    return lax.dot_general(a, b, dims, preferred_element_type=F32)


def swap_halves(x):
    return pltpu.roll(x, HALF, 1)


def low_lanes(rows):
    return lax.broadcasted_iota(jnp.int32, (rows, LANES), 1) < HALF


def turn(index, by):
    return lax.rem(index + by, SIDE)


def start_all(copies):
    for copy in copies:
        copy.start()
    return copies


def wait_all(copies):
    for copy in copies:
        copy.wait()


def add(*terms):
    total = terms[0].astype(F32)
    for term in terms[1:]:
        total = total + term.astype(F32)
    return total.astype(BF16)


def cut_for_column(grad, target, sems, y, x, by, split):
    to_x = turn(x, by)
    copies = [
        pltpu.make_async_copy(
            grad.at[k, to_x, :, pl.ds(0, split)], target.at[:, pl.ds(k * split, split)], sems.at[k]
        )
        for k in range(SIDE)
    ]
    rest = grad.shape[3] - split
    copies.append(
        pltpu.make_async_copy(
            grad.at[turn(y, 2), to_x, :, pl.ds(split, rest)], target.at[:, pl.ds(SIDE * split, rest)], sems.at[SIDE]
        )
    )
    return copies


def cut_for_row(grad, target, sem, y, by, split):
    rest = grad.shape[3] - split
    return [pltpu.make_async_copy(grad.at[turn(y, by), :, :, pl.ds(split, rest)], target, sem)]


def first_send_kernel(split, here, grad, a1, b1, a3, b3, a2, column_sems, row_sems):
    y, x = here[0], here[1]
    copies = []
    for k, (by, target) in enumerate(((1, a1), (3, a3), (2, a2))):
        copies += cut_for_column(grad, target, column_sems.at[k], y, x, by, split)
    for k, (by, target) in enumerate(((1, b1), (3, b3))):
        copies += cut_for_row(grad, target, row_sems.at[k], y, by, split)
    wait_all(start_all(copies))


def fetch(source, target, sems):
    return start_all(
        [
            pltpu.make_async_copy(source.at[slot], target.at[slot], sems.at[slot])
            for slot in range(source.shape[0])
        ]
    )


def second_send_kernel(
    split, here, grad, a1, b1, a3, b3, a2, p0, p1, p2, p3, q0, q1, q2, q3, own_a, own_b, column_sems, row_sems
):
    y, x = here[0], here[1]
    column = start_all(cut_for_column(grad, own_a, column_sems, y, x, 0, split))
    row = start_all(cut_for_row(grad, own_b, row_sems.at[0], y, 0, split))
    wait_all(column)
    for by, out in enumerate((p0, p1, p2, p3)):
        lanes = pl.ds(pl.multiple_of(turn(y, by) * split, split), split)
        out[:, :split] = add(own_a[:, lanes], a1[:, lanes], a3[:, lanes], a2[:, lanes])
    p2[:, split:] = add(*(ref[:, SIDE * split :] for ref in (own_a, a1, a3, a2)))
    wait_all(row)
    for by, out in enumerate((q0, q1, q2, q3)):
        to_x = turn(x, by)
        out[...] = add(own_b[to_x], b1[to_x], b3[to_x])


def outgoing_kernel(holder, p0, p1, p3, p2, q0, q1, q3, q2, out, flat):
    order = out.shape[2]
    first_blocks = p0.shape[1] // order
    for block in range(flat.shape[0]):
        lanes = slice(block * order, (block + 1) * order)
        if block < first_blocks:
            flat[block] = add(p0[:, lanes], p1[:, lanes], p2[:, lanes], p3[:, lanes])
        else:
            rest = slice((block - first_blocks) * order, (block - first_blocks + 1) * order)
            flat[block] = add(q0[:, rest], q1[:, rest], q2[:, rest], q3[:, rest], p2[:, lanes])
    for slot in range(out.shape[0]):
        out[slot] = flat[holder[slot]]


def moment_right_kernel(moment_hbm, second_hbm, basis_hbm, packed, moment, second, basis, small_sems, sems):
    small = start_all(
        [
            pltpu.make_async_copy(moment_hbm, moment, small_sems.at[0]),
            pltpu.make_async_copy(second_hbm, second, small_sems.at[1]),
        ]
    )
    arrivals = fetch(basis_hbm, basis, sems)
    wait_all(small)
    low = low_lanes(HALF)
    for slot in range(moment.shape[0]):
        arrivals[slot].wait()
        turned = dot(moment[slot], basis[slot], NN)
        for pair in range(packed.shape[0] // 2):
            lanes = slice(pair * LANES, (pair + 1) * LANES)
            a = turned[:, lanes]
            b = second[slot, :, lanes].astype(F32)
            packed[2 * pair, slot] = jnp.where(low, a, swap_halves(b)).astype(BF16)
            packed[2 * pair + 1, slot] = jnp.where(low, swap_halves(a), b).astype(BF16)


def moment_left_kernel(packed, basis_hbm, out, basis, sems):
    arrivals = fetch(basis_hbm, basis, sems)
    order = basis.shape[1]
    for slot in range(out.shape[0]):
        both = packed[:, slot].reshape(order, LANES)
        out[slot, HALF:] = both.astype(F32).T[HALF:]
        arrivals[slot].wait()
        out[slot, :HALF] = dot(both[:, :HALF], basis[slot], TN)


def rotate_right_kernel(used, rows, moment_hbm, basis_hbm, first, packed, moment, basis, small_sems, sems):
    small = pltpu.make_async_copy(moment_hbm, moment, small_sems.at[0])
    arrivals = fetch(basis_hbm, basis, sems)
    small.start()
    small.wait()
    half = HALF // 2
    low = low_lanes(half)
    for slot in range(rows.shape[0]):
        grad = rows[slot]
        mixed = BETA_FIRST * moment[slot].astype(F32) + (1.0 - BETA_FIRST) * grad.astype(F32)
        first[slot] = jnp.where(used[slot] > 0, mixed, 0.0).astype(BF16)
    for slot in range(rows.shape[0]):
        arrivals[slot].wait()
        turned = dot(rows[slot], basis[slot], NN)
        for pair in range(packed.shape[0] // 2):
            lanes = slice(pair * LANES, (pair + 1) * LANES)
            a = turned[:half, lanes]
            b = turned[half:, lanes]
            packed[2 * pair, slot] = jnp.where(low, a, swap_halves(b)).astype(BF16)
            packed[2 * pair + 1, slot] = jnp.where(low, swap_halves(a), b).astype(BF16)


def rotate_left_kernel(packed, basis_hbm, ready, out, basis, sems):
    arrivals = fetch(basis_hbm, basis, sems)
    order = basis.shape[1]
    parts, half = packed.shape[0], packed.shape[2]
    for slot in range(out.shape[1]):
        both = packed[:, slot].reshape(parts * half, LANES)
        arrivals[slot].wait()
        cut = basis[slot].reshape(parts, 2, half, order)
        rot_grad = dot(both[:, :HALF], cut[:, 0].reshape(parts * half, order), TN) + dot(
            both[:, HALF:], cut[:, 1].reshape(parts * half, order), TN
        )
        rot_mom = BETA_FIRST * ready[slot, :HALF] + (1.0 - BETA_FIRST) * rot_grad
        variance = BETA_SECOND * ready[slot, HALF:] + (1.0 - BETA_SECOND) * rot_grad * rot_grad
        direction = (rot_mom / (jnp.sqrt(variance) + EPSILON)).astype(BF16)
        step = dot(direction, basis[slot], NT)
        joined = jnp.concatenate([step, variance], axis=0).T.astype(BF16)
        out[:, slot] = joined.reshape(parts, HALF, LANES)


def step_kernel(used, packed, basis_hbm, second, step, basis, sems):
    arrivals = fetch(basis_hbm, basis, sems)
    low = low_lanes(HALF)
    for slot in range(second.shape[0]):
        lefts = []
        for pair in range(packed.shape[0] // 2):
            lanes = slice(pair * LANES, (pair + 1) * LANES)
            a = packed[2 * pair, slot].astype(F32)
            b = packed[2 * pair + 1, slot].astype(F32)
            lefts.append(jnp.where(low, a, swap_halves(b)).astype(BF16))
            v = jnp.where(low, swap_halves(a), b)
            second[slot, :, lanes] = jnp.where(used[slot] > 0, v, 0.0).astype(BF16)
        arrivals[slot].wait()
        moved = dot(jnp.concatenate(lefts, axis=1), basis[slot], NT)
        step[:, slot] = moved.reshape(step.shape[0], step.shape[2], step.shape[3]).astype(BF16)


def gram_tiles_kernel(
    here, rows, y2, x2, y1, y3, x1,
    own, left0, left1, left2, left3, right0, right1, right2, right3,
    across, down, grams, sems,
):
    y, x = here[0], here[1]
    slots, slab, order = rows.shape
    lines = SIDE * slab
    start = pl.multiple_of(y * lines, lines)
    copies = []
    for back, ref in enumerate((x1, x2)):
        copies.append(pltpu.make_async_copy(ref, across.at[back], sems.at[0, back]))
    for back, ref in enumerate((rows, y1, y2, y3)):
        copies.append(pltpu.make_async_copy(ref, down.at[back], sems.at[1, back]))
    wait_all(start_all(copies))
    for slot in range(slots):
        panel = down[:, slot].reshape(lines, order)
        tile = dot(panel, across[:, slot].reshape(2 * slab, order), NT)
        own[slot] = dot(down[0, slot], panel, NT)
        for back, out in enumerate((left0, left1, left2, left3)):
            out[slot] = tile[back * slab : (back + 1) * slab].astype(out.dtype)
        columns = down[:, slot, :, pl.ds(start, lines)].reshape(lines, lines)
        grams[...] = dot(columns, panel, TN).reshape(grams.shape)
        for by, out in enumerate((right0, right1, right2, right3)):
            out[slot, :, :order] = grams[turn(x, by)].astype(out.dtype)
        right3[slot, :, order:] = dot(across[0, slot], panel, NT).astype(BF16)


def spread(pair, which):
    other = swap_halves(pair)
    low = low_lanes(pair.shape[0])
    twice = jnp.where(low, pair, other) if which == 0 else jnp.where(low, other, pair)
    return jnp.concatenate([twice, twice], axis=1)


def gram_sum_kernel(
    here, used, own, left0, left1, left2, left3, right0, right1, right2, right3, left_hbm, right_hbm,
    new_left, new_right, left, right, sems,
):
    y, x = here[0], here[1]
    old = start_all(
        [pltpu.make_async_copy(left_hbm, left, sems.at[0]), pltpu.make_async_copy(right_hbm, right, sems.at[1])]
    )
    slots, slab, order = left.shape
    lines = own.shape[2]
    column = lax.broadcasted_iota(jnp.int32, (slab, lines), 1) // HALF
    wait_all(old)
    for slot in range(slots):
        is_used = used[slot] > 0
        for ahead, tile in enumerate((left0, left1, left2, left3)):
            back = (SIDE - ahead) % SIDE
            same = spread(own[slot, :, back // 2 * LANES :][:, :LANES], back % 2)
            first = order + back // 2 * LANES
            ahead_x = spread(right3[slot, :, first : first + LANES].astype(F32), back % 2)
            tile = tile[slot].astype(F32)
            gram = jnp.where(column == turn(x, 1), ahead_x, same)
            gram = jnp.where(column == turn(x, 3), spread(tile, 0), gram)
            gram = jnp.where(column == turn(x, 2), spread(tile, 1), gram)
            lanes = pl.ds(pl.multiple_of(turn(y, ahead) * lines, lines), lines)
            new_left[slot, :, lanes] = jnp.where(
                is_used, BETA_FACTOR * left[slot, :, lanes] + (1.0 - BETA_FACTOR) * gram, 0.0
            )
        gram = right0[slot]
        for term in (right1, right2, right3):
            gram = gram + term[slot, :, :order].astype(F32)
        new_right[slot] = jnp.where(is_used, BETA_FACTOR * right[slot] + (1.0 - BETA_FACTOR) * gram, 0.0)


def along_x(value, by):
    pairs = [
        (y * SIDE + x, y * SIDE + (x + by) % SIDE) for y in range(SIDE) for x in range(SIDE)
    ]
    return lax.ppermute(value, "dp", pairs)


def along_y(value, by):
    pairs = [
        (y * SIDE + x, ((y + by) % SIDE) * SIDE + x) for y in range(SIDE) for x in range(SIDE)
    ]
    return lax.ppermute(value, "dp", pairs)


def call(kernel, name, ins, outs, scratch, products, moved):
    arrays = [pltpu.with_memory_space_constraint(array, space) if space == HBM else array for array, space in ins]
    return pl.pallas_call(
        kernel,
        in_specs=[pl.BlockSpec(memory_space=space) for _, space in ins],
        out_specs=[pl.BlockSpec(memory_space=space or VMEM) for _, _, space in outs],
        out_shape=[
            space(shape, dtype) if space == VMEM else jax.ShapeDtypeStruct(shape, dtype) for shape, dtype, space in outs
        ],
        scratch_shapes=scratch,
        compiler_params=pltpu.CompilerParams(vmem_limit_bytes=VMEM_BYTES),
        cost_estimate=pl.CostEstimate(flops=products * 2**27, bytes_accessed=moved * 2**20, transcendentals=0),
        name=name,
    )(*arrays)


def sum_replicas(grad, here, holder, slot_total, order, beside, between):
    rows, width = grad.shape[1], grad.shape[2]
    split = width // order // 6 * order
    rest = width - split
    grad = grad.reshape(SIDE, SIDE, rows, width)
    column, row = (rows, SIDE * split + rest), (SIDE, rows, rest)
    sent = call(
        functools.partial(first_send_kernel, split), "first_send", [(here, SMEM), (grad, HBM)],
        [(shape, BF16, VMEM) for shape in (column, row, column, row, column)],
        [pltpu.SemaphoreType.DMA((3, SIDE + 1)), pltpu.SemaphoreType.DMA((2,))], 0, 5,
    )
    got = [along_x(sent[0], 1), along_y(sent[1], 1), along_x(sent[2], 3), along_y(sent[3], 3), along_x(sent[4], 2)]
    got, early = lax.optimization_barrier((got, beside()))
    early = between(early)
    piece, piece_rest, both = (rows, split), (rows, rest), (rows, width)
    pieces = call(
        functools.partial(second_send_kernel, split), "second_send",
        [(here, SMEM), (grad, HBM)] + [(value, VMEM) for value in got],
        [(piece, BF16, None), (piece, BF16, VMEM), (both, BF16, VMEM), (piece, BF16, VMEM), (piece_rest, BF16, None)]
        + [(piece_rest, BF16, VMEM)] * 3,
        [
            pltpu.VMEM(column, BF16), pltpu.VMEM(row, BF16), pltpu.SemaphoreType.DMA((SIDE + 1,)),
            pltpu.SemaphoreType.DMA((1,)),
        ],
        0, 4,
    )
    p, q = [pieces[0]], [pieces[4]]
    for by in (1, 3, 2):
        p.append(along_y(pieces[by], by))
        q.append(along_x(pieces[4 + by], by))
    p, q, early = lax.optimization_barrier((p, q, early))
    outgoing = call(
        outgoing_kernel, "outgoing", [(holder, SMEM)] + [(value, VMEM) for value in p + q],
        [((slot_total, rows, order), BF16, VMEM)], [pltpu.VMEM((width // order, rows, order), BF16)], 0, 1,
    )[0]
    return outgoing, early


def on_device(
    grad_part,
    block_slot,
    left_factor,
    right_factor,
    first_moment,
    second_moment,
    left_basis,
    right_basis,
):
    owners = lax.axis_size("owner")
    replicas = lax.axis_size("dp")
    mine_dp = lax.axis_index("dp").astype(jnp.int32)
    mine_owner = lax.axis_index("owner")
    slots, slab, order = left_factor.shape
    part_rows = grad_part.shape[2]
    width = grad_part.shape[3]
    blocks = width // order

    slot_ids = jnp.arange(owners * slots, dtype=jnp.int32)
    matches = block_slot[None, :] == slot_ids[:, None]
    filled = jnp.any(matches, axis=1).astype(jnp.int32)
    holder = jnp.sum(jnp.where(matches, jnp.arange(blocks, dtype=jnp.int32)[None, :], 0), axis=1)
    used = lax.dynamic_slice_in_dim(filled, mine_owner * slots, slots)
    here = jnp.stack([mine_dp // SIDE, mine_dp % SIDE])

    slabs = (slots, slab, order)

    def exchange(value, axis):
        return lax.all_to_all(value, axis, split_axis=0, concat_axis=0, tiled=True)

    basis_scratch = [pltpu.VMEM((slots, order, order), BF16), pltpu.SemaphoreType.DMA((slots,))]
    chunks = (replicas, slots, slab, LANES)

    def moment_right():
        return call(
            moment_right_kernel, "moment_right",
            [(first_moment, HBM), (second_moment, HBM), (right_basis, HBM)], [(chunks, BF16, VMEM)],
            [pltpu.VMEM(slabs, BF16), pltpu.VMEM(slabs, BF16), basis_scratch[0], pltpu.SemaphoreType.DMA((2,)), basis_scratch[1]],
            3, 8,
        )[0]

    outgoing, early = sum_replicas(
        grad_part[0], here, holder, owners * slots, order, moment_right, lambda value: exchange(value, "dp")
    )
    incoming = exchange(outgoing.reshape(owners, slots, part_rows, order), "owner")
    ready = call(
        moment_left_kernel, "moment_left", [(early, VMEM), (left_basis, HBM)],
        [((slots, 2 * slab, order), F32, VMEM)], basis_scratch, 3, 8,
    )[0]
    incoming, ready = lax.optimization_barrier((incoming, ready))
    rows = incoming.transpose(1, 0, 2, 3).reshape(slabs)

    new_first, packed = call(
        rotate_right_kernel, "rotate_right",
        [(used, SMEM), (rows, VMEM), (first_moment, HBM), (right_basis, HBM)],
        [(slabs, BF16, None), ((replicas, slots, slab // 2, LANES), BF16, VMEM)],
        [pltpu.VMEM(slabs, BF16), basis_scratch[0], pltpu.SemaphoreType.DMA((1,)), basis_scratch[1]], 3, 8,
    )
    rows, packed = lax.optimization_barrier((rows, packed))
    packed = exchange(packed, "dp")
    near = [along_y(rows, 2), along_x(rows, 2), along_y(rows, 1), along_y(rows, 3), along_x(rows, 1)]
    turned = call(
        rotate_left_kernel, "rotate_left", [(packed, VMEM), (left_basis, HBM), (ready, VMEM)],
        [(chunks, BF16, VMEM)], basis_scratch, 9, 8,
    )[0]
    near, turned = lax.optimization_barrier((near, turned))
    turned = exchange(turned, "dp")
    tiles = call(
        gram_tiles_kernel, "gram_tiles", [(here, SMEM)] + [(value, HBM) for value in [rows] + near],
        [((slots, slab, SIDE * slab), F32, VMEM)]
        + [((slots, slab, 2 * slab), F32 if k == 0 else BF16, VMEM) for k in range(SIDE)]
        + [(slabs, F32, VMEM), (slabs, BF16, VMEM), (slabs, BF16, VMEM), ((slots, slab, order + SIDE * slab), BF16, VMEM)],
        [
            pltpu.VMEM((2, slots, slab, order), BF16), pltpu.VMEM((SIDE, slots, slab, order), BF16),
            pltpu.VMEM((SIDE, slab, order), F32), pltpu.SemaphoreType.DMA((2, SIDE)),
        ],
        9, 6,
    )
    lefts = [tiles[1]] + [along_y(tiles[1 + back], SIDE - back) for back in (1, 2, 3)]
    rights = [tiles[1 + SIDE]] + [along_x(tiles[1 + SIDE + by], by) for by in (1, 2, 3)]
    early_lefts, turned = lax.optimization_barrier((lefts[1:3], turned))
    lefts = [lefts[0], *early_lefts, lefts[3]]
    new_second, step = call(
        step_kernel, "step_rows", [(used, SMEM), (turned, VMEM), (right_basis, HBM)],
        [(slabs, BF16, None), ((owners, slots, part_rows, order), BF16, VMEM)], basis_scratch, 3, 8,
    )
    returned = exchange(step, "owner")
    rights, step = lax.optimization_barrier((rights, step))
    new_left, new_right = call(
        gram_sum_kernel, "gram_sum",
        [(here, SMEM), (used, SMEM)] + [(value, VMEM) for value in [tiles[0]] + lefts + rights]
        + [(left_factor, HBM), (right_factor, HBM)],
        [(slabs, F32, None)] * 2,
        [pltpu.VMEM(slabs, F32), pltpu.VMEM(slabs, F32), pltpu.SemaphoreType.DMA((2,))], 0, 8,
    )

    picked = returned.reshape(owners * slots, part_rows, order).at[block_slot].get(mode="promise_in_bounds")
    update = picked.transpose(1, 0, 2).reshape(part_rows, width)
    return new_left, new_right, new_first, new_second, update


def solution(mesh):
    slabs = P("owner", "dp", None)
    whole_slots = P("owner", None, None)
    return jax.shard_map(
        on_device,
        mesh=mesh,
        in_specs=(
            P("dp", None, "owner", None),
            P(),
            slabs,
            slabs,
            slabs,
            slabs,
            whole_slots,
            whole_slots,
        ),
        out_specs=(slabs, slabs, slabs, slabs, P(("dp", "owner"), None)),
        check_vma=False,
    )
```

```python
import functools

import jax
import jax.numpy as jnp
from jax import lax
from jax.experimental import pallas as pl
from jax.experimental.pallas import tpu as pltpu
from jax.sharding import PartitionSpec as P

BETA_FIRST = 0.9
BETA_SECOND = 0.95
BETA_FACTOR = 0.95
EPSILON = 1e-08
F32 = jnp.float32
BF16 = jnp.bfloat16
HALF = 64
LANES = 128
VMEM_BYTES = 32 * 1024 * 1024
SMEM, VMEM, HBM, ANY = pltpu.SMEM, pltpu.VMEM, pltpu.HBM, pl.ANY
SIDE = 4

NN = (((1,), (0,)), ((), ()))
NT = (((1,), (1,)), ((), ()))
TN = (((0,), (0,)), ((), ()))


def dot(a, b, dims):
    return lax.dot_general(a, b, dims, preferred_element_type=F32)


def swap_halves(x):
    return pltpu.roll(x, HALF, 1)


def low_lanes(rows):
    return lax.broadcasted_iota(jnp.int32, (rows, LANES), 1) < HALF


def turn(index, by):
    return lax.rem(index + by, SIDE)


def start_all(copies):
    for copy in copies:
        copy.start()
    return copies


def wait_all(copies):
    for copy in copies:
        copy.wait()


def add(*terms):
    total = terms[0].astype(F32)
    for term in terms[1:]:
        total = total + term.astype(F32)
    return total.astype(BF16)


def cut_for_column(grad, target, sems, y, x, by, split):
    to_x = turn(x, by)
    copies = [
        pltpu.make_async_copy(
            grad.at[k, to_x, :, pl.ds(0, split)], target.at[:, pl.ds(k * split, split)], sems.at[k]
        )
        for k in range(SIDE)
    ]
    rest = grad.shape[3] - split
    copies.append(
        pltpu.make_async_copy(
            grad.at[turn(y, 2), to_x, :, pl.ds(split, rest)], target.at[:, pl.ds(SIDE * split, rest)], sems.at[SIDE]
        )
    )
    return copies


def cut_for_row(grad, target, sem, y, by, split):
    rest = grad.shape[3] - split
    return [pltpu.make_async_copy(grad.at[turn(y, by), :, :, pl.ds(split, rest)], target, sem)]


def first_send_kernel(split, here, grad, a1, b1, a3, b3, a2, column_sems, row_sems):
    y, x = here[0], here[1]
    copies = []
    for k, (by, target) in enumerate(((1, a1), (3, a3), (2, a2))):
        copies += cut_for_column(grad, target, column_sems.at[k], y, x, by, split)
    for k, (by, target) in enumerate(((1, b1), (3, b3))):
        copies += cut_for_row(grad, target, row_sems.at[k], y, by, split)
    wait_all(start_all(copies))


def fetch(source, target, sems):
    return start_all(
        [
            pltpu.make_async_copy(source.at[slot], target.at[slot], sems.at[slot])
            for slot in range(source.shape[0])
        ]
    )


def second_send_kernel(
    split, here, grad, a1, b1, a3, b3, a2, p0, p1, p2, p3, q0, q1, q2, q3, own_a, own_b, column_sems, row_sems
):
    y, x = here[0], here[1]
    column = start_all(cut_for_column(grad, own_a, column_sems, y, x, 0, split))
    row = start_all(cut_for_row(grad, own_b, row_sems.at[0], y, 0, split))
    wait_all(column)
    for by, out in enumerate((p0, p1, p2, p3)):
        lanes = pl.ds(pl.multiple_of(turn(y, by) * split, split), split)
        out[:, :split] = add(own_a[:, lanes], a1[:, lanes], a3[:, lanes], a2[:, lanes])
    p2[:, split:] = add(*(ref[:, SIDE * split :] for ref in (own_a, a1, a3, a2)))
    wait_all(row)
    for by, out in enumerate((q0, q1, q2, q3)):
        to_x = turn(x, by)
        out[...] = add(own_b[to_x], b1[to_x], b3[to_x])


def outgoing_kernel(holder, p0, p1, p3, p2, q0, q1, q3, q2, out, flat):
    order = out.shape[2]
    first_blocks = p0.shape[1] // order
    for block in range(flat.shape[0]):
        lanes = slice(block * order, (block + 1) * order)
        if block < first_blocks:
            flat[block] = add(p0[:, lanes], p1[:, lanes], p2[:, lanes], p3[:, lanes])
        else:
            rest = slice((block - first_blocks) * order, (block - first_blocks + 1) * order)
            flat[block] = add(q0[:, rest], q1[:, rest], q2[:, rest], q3[:, rest], p2[:, lanes])
    for slot in range(out.shape[0]):
        out[slot] = flat[holder[slot]]


def moment_right_kernel(moment_hbm, second_hbm, basis_hbm, packed, moment, second, basis, small_sems, sems):
    small = start_all(
        [
            pltpu.make_async_copy(moment_hbm, moment, small_sems.at[0]),
            pltpu.make_async_copy(second_hbm, second, small_sems.at[1]),
        ]
    )
    arrivals = fetch(basis_hbm, basis, sems)
    wait_all(small)
    low = low_lanes(HALF)
    for slot in range(moment.shape[0]):
        arrivals[slot].wait()
        turned = dot(moment[slot], basis[slot], NN)
        for pair in range(packed.shape[0] // 2):
            lanes = slice(pair * LANES, (pair + 1) * LANES)
            a = turned[:, lanes]
            b = second[slot, :, lanes].astype(F32)
            packed[2 * pair, slot] = jnp.where(low, a, swap_halves(b)).astype(BF16)
            packed[2 * pair + 1, slot] = jnp.where(low, swap_halves(a), b).astype(BF16)


def moment_left_kernel(packed, basis_hbm, out, basis, sems):
    arrivals = fetch(basis_hbm, basis, sems)
    order = basis.shape[1]
    for slot in range(out.shape[0]):
        both = packed[:, slot].reshape(order, LANES)
        out[slot, HALF:] = both.astype(F32).T[HALF:]
        arrivals[slot].wait()
        out[slot, :HALF] = dot(both[:, :HALF], basis[slot], TN)


def rotate_right_kernel(used, rows, moment_hbm, basis_hbm, first_hbm, packed, moment, first, basis, small_sems, sems):
    small = pltpu.make_async_copy(moment_hbm, moment, small_sems.at[0])
    arrivals = fetch(basis_hbm, basis, sems)
    small.start()
    small.wait()
    half = HALF // 2
    low = low_lanes(half)
    for slot in range(rows.shape[0]):
        grad = rows[slot]
        mixed = BETA_FIRST * moment[slot].astype(F32) + (1.0 - BETA_FIRST) * grad.astype(F32)
        first[slot] = jnp.where(used[slot] > 0, mixed, 0.0).astype(BF16)
    done = pltpu.make_async_copy(first, first_hbm, small_sems.at[1])
    done.start()
    for slot in range(rows.shape[0]):
        arrivals[slot].wait()
        turned = dot(rows[slot], basis[slot], NN)
        for pair in range(packed.shape[0] // 2):
            lanes = slice(pair * LANES, (pair + 1) * LANES)
            a = turned[:half, lanes]
            b = turned[half:, lanes]
            packed[2 * pair, slot] = jnp.where(low, a, swap_halves(b)).astype(BF16)
            packed[2 * pair + 1, slot] = jnp.where(low, swap_halves(a), b).astype(BF16)
    done.wait()


def rotate_left_kernel(packed, basis_hbm, ready, out, basis, sems):
    arrivals = fetch(basis_hbm, basis, sems)
    order = basis.shape[1]
    parts, half = packed.shape[0], packed.shape[2]
    for slot in range(out.shape[1]):
        both = packed[:, slot].reshape(parts * half, LANES)
        arrivals[slot].wait()
        cut = basis[slot].reshape(parts, 2, half, order)
        rot_grad = dot(both[:, :HALF], cut[:, 0].reshape(parts * half, order), TN) + dot(
            both[:, HALF:], cut[:, 1].reshape(parts * half, order), TN
        )
        rot_mom = BETA_FIRST * ready[slot, :HALF] + (1.0 - BETA_FIRST) * rot_grad
        variance = BETA_SECOND * ready[slot, HALF:] + (1.0 - BETA_SECOND) * rot_grad * rot_grad
        direction = (rot_mom / (jnp.sqrt(variance) + EPSILON)).astype(BF16)
        step = dot(direction, basis[slot], NT)
        joined = jnp.concatenate([step, variance], axis=0).T.astype(BF16)
        out[:, slot] = joined.reshape(parts, HALF, LANES)


def step_kernel(used, packed, basis_hbm, second_hbm, step, basis, second, sems, out_sems):
    arrivals = fetch(basis_hbm, basis, sems)
    low = low_lanes(HALF)
    done = []
    for slot in range(second.shape[0]):
        lefts = []
        for pair in range(packed.shape[0] // 2):
            lanes = slice(pair * LANES, (pair + 1) * LANES)
            a = packed[2 * pair, slot].astype(F32)
            b = packed[2 * pair + 1, slot].astype(F32)
            lefts.append(jnp.where(low, a, swap_halves(b)).astype(BF16))
            v = jnp.where(low, swap_halves(a), b)
            second[slot, :, lanes] = jnp.where(used[slot] > 0, v, 0.0).astype(BF16)
        done.append(pltpu.make_async_copy(second.at[slot], second_hbm.at[slot], out_sems.at[slot]))
        done[slot].start()
        arrivals[slot].wait()
        moved = dot(jnp.concatenate(lefts, axis=1), basis[slot], NT)
        step[:, slot] = moved.reshape(step.shape[0], step.shape[2], step.shape[3]).astype(BF16)
    wait_all(done)


def gram_tiles_kernel(
    here, rows, y2, x2, y1, y3, x1,
    own, left0, left1, left2, left3, right0, right1, right2, right3,
    across, down, grams, sems,
):
    y, x = here[0], here[1]
    slots, slab, order = rows.shape
    lines = SIDE * slab
    start = pl.multiple_of(y * lines, lines)
    copies = []
    for back, ref in enumerate((x1, x2)):
        copies.append(pltpu.make_async_copy(ref, across.at[back], sems.at[0, back]))
    for back, ref in enumerate((rows, y1, y2, y3)):
        copies.append(pltpu.make_async_copy(ref, down.at[back], sems.at[1, back]))
    wait_all(start_all(copies))
    for slot in range(slots):
        panel = down[:, slot].reshape(lines, order)
        tile = dot(panel, across[:, slot].reshape(2 * slab, order), NT)
        own[slot] = dot(down[0, slot], panel, NT)
        for back, out in enumerate((left0, left1, left2, left3)):
            out[slot] = tile[back * slab : (back + 1) * slab].astype(out.dtype)
        columns = down[:, slot, :, pl.ds(start, lines)].reshape(lines, lines)
        grams[...] = dot(columns, panel, TN).reshape(grams.shape)
        for by, out in enumerate((right0, right1, right2, right3)):
            out[slot, :, :order] = grams[turn(x, by)].astype(out.dtype)
        right3[slot, :, order:] = dot(across[0, slot], panel, NT).astype(BF16)


def spread(pair, which):
    other = swap_halves(pair)
    low = low_lanes(pair.shape[0])
    twice = jnp.where(low, pair, other) if which == 0 else jnp.where(low, other, pair)
    return jnp.concatenate([twice, twice], axis=1)


def gram_sum_kernel(
    here, used, own, left0, left1, left2, left3, right0, right1, right2, right3, left_hbm, right_hbm,
    new_left_hbm, new_right_hbm, left, right, sems, out_sems,
):
    y, x = here[0], here[1]
    slots, slab, order = left.shape
    old = [
        start_all(
            [
                pltpu.make_async_copy(right_hbm.at[slot], right.at[slot], sems.at[slot, 0]),
                pltpu.make_async_copy(left_hbm.at[slot], left.at[slot], sems.at[slot, 1]),
            ]
        )
        for slot in range(slots)
    ]
    done = []
    lines = own.shape[2]
    column = lax.broadcasted_iota(jnp.int32, (slab, lines), 1) // HALF
    for slot in range(slots):
        is_used = used[slot] > 0
        wait_all(old[slot])
        for ahead, tile in enumerate((left0, left1, left2, left3)):
            back = (SIDE - ahead) % SIDE
            same = spread(own[slot, :, back // 2 * LANES :][:, :LANES], back % 2)
            first = order + back // 2 * LANES
            ahead_x = spread(right3[slot, :, first : first + LANES].astype(F32), back % 2)
            tile = tile[slot].astype(F32)
            gram = jnp.where(column == turn(x, 1), ahead_x, same)
            gram = jnp.where(column == turn(x, 3), spread(tile, 0), gram)
            gram = jnp.where(column == turn(x, 2), spread(tile, 1), gram)
            lanes = pl.ds(pl.multiple_of(turn(y, ahead) * lines, lines), lines)
            left[slot, :, lanes] = jnp.where(
                is_used, BETA_FACTOR * left[slot, :, lanes] + (1.0 - BETA_FACTOR) * gram, 0.0
            )
        gram = right0[slot]
        for term in (right1, right2, right3):
            gram = gram + term[slot, :, :order].astype(F32)
        right[slot] = jnp.where(is_used, BETA_FACTOR * right[slot] + (1.0 - BETA_FACTOR) * gram, 0.0)
        done += start_all(
            [
                pltpu.make_async_copy(right.at[slot], new_right_hbm.at[slot], out_sems.at[slot, 0]),
                pltpu.make_async_copy(left.at[slot], new_left_hbm.at[slot], out_sems.at[slot, 1]),
            ]
        )
    wait_all(done)


def along_x(value, by):
    pairs = [
        (y * SIDE + x, y * SIDE + (x + by) % SIDE) for y in range(SIDE) for x in range(SIDE)
    ]
    return lax.ppermute(value, "dp", pairs)


def along_y(value, by):
    pairs = [
        (y * SIDE + x, ((y + by) % SIDE) * SIDE + x) for y in range(SIDE) for x in range(SIDE)
    ]
    return lax.ppermute(value, "dp", pairs)


def call(kernel, name, ins, outs, scratch, products, moved):
    arrays = [pltpu.with_memory_space_constraint(array, space) if space == HBM else array for array, space in ins]
    return pl.pallas_call(
        kernel,
        in_specs=[pl.BlockSpec(memory_space=space) for _, space in ins],
        out_specs=[pl.BlockSpec(memory_space=space or VMEM) for _, _, space in outs],
        out_shape=[
            space(shape, dtype) if space == VMEM else jax.ShapeDtypeStruct(shape, dtype) for shape, dtype, space in outs
        ],
        scratch_shapes=scratch,
        compiler_params=pltpu.CompilerParams(vmem_limit_bytes=VMEM_BYTES),
        cost_estimate=pl.CostEstimate(flops=products * 2**27, bytes_accessed=moved * 2**20, transcendentals=0),
        name=name,
    )(*arrays)


def sum_replicas(grad, here, holder, slot_total, order, beside, between):
    rows, width = grad.shape[1], grad.shape[2]
    split = width // order // 6 * order
    rest = width - split
    grad = grad.reshape(SIDE, SIDE, rows, width)
    column, row = (rows, SIDE * split + rest), (SIDE, rows, rest)
    sent = call(
        functools.partial(first_send_kernel, split), "first_send", [(here, SMEM), (grad, HBM)],
        [(shape, BF16, VMEM) for shape in (column, row, column, row, column)],
        [pltpu.SemaphoreType.DMA((3, SIDE + 1)), pltpu.SemaphoreType.DMA((2,))], 0, 5,
    )
    got = [along_x(sent[0], 1), along_y(sent[1], 1), along_x(sent[2], 3), along_y(sent[3], 3), along_x(sent[4], 2)]
    got, early = lax.optimization_barrier((got, beside()))
    early = between(early)
    piece, piece_rest, both = (rows, split), (rows, rest), (rows, width)
    pieces = call(
        functools.partial(second_send_kernel, split), "second_send",
        [(here, SMEM), (grad, HBM)] + [(value, VMEM) for value in got],
        [(piece, BF16, None), (piece, BF16, VMEM), (both, BF16, VMEM), (piece, BF16, VMEM), (piece_rest, BF16, None)]
        + [(piece_rest, BF16, VMEM)] * 3,
        [
            pltpu.VMEM(column, BF16), pltpu.VMEM(row, BF16), pltpu.SemaphoreType.DMA((SIDE + 1,)),
            pltpu.SemaphoreType.DMA((1,)),
        ],
        0, 4,
    )
    p, q = [pieces[0]], [pieces[4]]
    for by in (1, 3, 2):
        p.append(along_y(pieces[by], by))
        q.append(along_x(pieces[4 + by], by))
    p, q, early = lax.optimization_barrier((p, q, early))
    outgoing = call(
        outgoing_kernel, "outgoing", [(holder, SMEM)] + [(value, VMEM) for value in p + q],
        [((slot_total, rows, order), BF16, VMEM)], [pltpu.VMEM((width // order, rows, order), BF16)], 0, 1,
    )[0]
    return outgoing, early


def on_device(
    grad_part,
    block_slot,
    left_factor,
    right_factor,
    first_moment,
    second_moment,
    left_basis,
    right_basis,
):
    owners = lax.axis_size("owner")
    replicas = lax.axis_size("dp")
    mine_dp = lax.axis_index("dp").astype(jnp.int32)
    mine_owner = lax.axis_index("owner")
    slots, slab, order = left_factor.shape
    part_rows = grad_part.shape[2]
    width = grad_part.shape[3]
    blocks = width // order

    slot_ids = jnp.arange(owners * slots, dtype=jnp.int32)
    matches = block_slot[None, :] == slot_ids[:, None]
    filled = jnp.any(matches, axis=1).astype(jnp.int32)
    holder = jnp.sum(jnp.where(matches, jnp.arange(blocks, dtype=jnp.int32)[None, :], 0), axis=1)
    used = lax.dynamic_slice_in_dim(filled, mine_owner * slots, slots)
    here = jnp.stack([mine_dp // SIDE, mine_dp % SIDE])

    slabs = (slots, slab, order)

    def exchange(value, axis):
        return lax.all_to_all(value, axis, split_axis=0, concat_axis=0, tiled=True)

    basis_scratch = [pltpu.VMEM((slots, order, order), BF16), pltpu.SemaphoreType.DMA((slots,))]
    chunks = (replicas, slots, slab, LANES)

    def moment_right():
        return call(
            moment_right_kernel, "moment_right",
            [(first_moment, HBM), (second_moment, HBM), (right_basis, HBM)], [(chunks, BF16, VMEM)],
            [pltpu.VMEM(slabs, BF16), pltpu.VMEM(slabs, BF16), basis_scratch[0], pltpu.SemaphoreType.DMA((2,)), basis_scratch[1]],
            3, 8,
        )[0]

    outgoing, early = sum_replicas(
        grad_part[0], here, holder, owners * slots, order, moment_right, lambda value: exchange(value, "dp")
    )
    incoming = exchange(outgoing.reshape(owners, slots, part_rows, order), "owner")
    ready = call(
        moment_left_kernel, "moment_left", [(early, VMEM), (left_basis, HBM)],
        [((slots, 2 * slab, order), F32, VMEM)], basis_scratch, 3, 8,
    )[0]
    incoming, ready = lax.optimization_barrier((incoming, ready))
    rows = incoming.transpose(1, 0, 2, 3).reshape(slabs)

    new_first, packed = call(
        rotate_right_kernel, "rotate_right",
        [(used, SMEM), (rows, VMEM), (first_moment, HBM), (right_basis, HBM)],
        [(slabs, BF16, HBM), ((replicas, slots, slab // 2, LANES), BF16, VMEM)],
        [pltpu.VMEM(slabs, BF16), pltpu.VMEM(slabs, BF16), basis_scratch[0], pltpu.SemaphoreType.DMA((2,)), basis_scratch[1]],
        3, 8,
    )
    rows, packed = lax.optimization_barrier((rows, packed))
    packed = exchange(packed, "dp")
    near = [along_y(rows, 2), along_x(rows, 2), along_y(rows, 1), along_y(rows, 3), along_x(rows, 1)]
    turned = call(
        rotate_left_kernel, "rotate_left", [(packed, VMEM), (left_basis, HBM), (ready, VMEM)],
        [(chunks, BF16, VMEM)], basis_scratch, 9, 8,
    )[0]
    near, turned = lax.optimization_barrier((near, turned))
    turned = exchange(turned, "dp")
    tiles = call(
        gram_tiles_kernel, "gram_tiles", [(here, SMEM)] + [(value, HBM) for value in [rows] + near],
        [((slots, slab, SIDE * slab), F32, VMEM)]
        + [((slots, slab, 2 * slab), F32 if k == 0 else BF16, VMEM) for k in range(SIDE)]
        + [(slabs, F32, VMEM), (slabs, BF16, VMEM), (slabs, BF16, VMEM), ((slots, slab, order + SIDE * slab), BF16, VMEM)],
        [
            pltpu.VMEM((2, slots, slab, order), BF16), pltpu.VMEM((SIDE, slots, slab, order), BF16),
            pltpu.VMEM((SIDE, slab, order), F32), pltpu.SemaphoreType.DMA((2, SIDE)),
        ],
        9, 6,
    )
    lefts = [tiles[1]] + [along_y(tiles[1 + back], SIDE - back) for back in (1, 2, 3)]
    rights = [tiles[1 + SIDE]] + [along_x(tiles[1 + SIDE + by], by) for by in (1, 2, 3)]
    early_lefts, turned = lax.optimization_barrier((lefts[1:2], turned))
    lefts = [lefts[0], *early_lefts, *lefts[2:]]
    new_second, step = call(
        step_kernel, "step_rows", [(used, SMEM), (turned, VMEM), (right_basis, HBM)],
        [(slabs, BF16, HBM), ((owners, slots, part_rows, order), BF16, VMEM)],
        [basis_scratch[0], pltpu.VMEM(slabs, BF16), basis_scratch[1], pltpu.SemaphoreType.DMA((slots,))], 3, 8,
    )
    returned = exchange(step, "owner")
    rights, step = lax.optimization_barrier((rights, step))
    new_left, new_right = call(
        gram_sum_kernel, "gram_sum",
        [(here, SMEM), (used, SMEM)] + [(value, VMEM) for value in [tiles[0]] + lefts + rights]
        + [(left_factor, HBM), (right_factor, HBM)],
        [(slabs, F32, HBM)] * 2,
        [
            pltpu.VMEM(slabs, F32), pltpu.VMEM(slabs, F32), pltpu.SemaphoreType.DMA((slots, 2)),
            pltpu.SemaphoreType.DMA((slots, 2)),
        ],
        0, 8,
    )

    picked = returned.reshape(owners * slots, part_rows, order).at[block_slot].get(mode="promise_in_bounds")
    update = picked.transpose(1, 0, 2).reshape(part_rows, width)
    return new_left, new_right, new_first, new_second, update


def solution(mesh):
    slabs = P("owner", "dp", None)
    whole_slots = P("owner", None, None)
    return jax.shard_map(
        on_device,
        mesh=mesh,
        in_specs=(
            P("dp", None, "owner", None),
            P(),
            slabs,
            slabs,
            slabs,
            slabs,
            whole_slots,
            whole_slots,
        ),
        out_specs=(slabs, slabs, slabs, slabs, P(("dp", "owner"), None)),
        check_vma=False,
    )
```

```python
import functools

import jax
import jax.numpy as jnp
from jax import lax
from jax.experimental import pallas as pl
from jax.experimental.pallas import tpu as pltpu
from jax.sharding import PartitionSpec as P

BETA_FIRST = 0.9
BETA_SECOND = 0.95
BETA_FACTOR = 0.95
EPSILON = 1e-08
F32 = jnp.float32
BF16 = jnp.bfloat16
HALF = 64
LANES = 128
VMEM_BYTES = 32 * 1024 * 1024
SMEM, VMEM, HBM, ANY = pltpu.SMEM, pltpu.VMEM, pltpu.HBM, pl.ANY
SIDE = 4

NN = (((1,), (0,)), ((), ()))
NT = (((1,), (1,)), ((), ()))
TN = (((0,), (0,)), ((), ()))


def dot(a, b, dims):
    return lax.dot_general(a, b, dims, preferred_element_type=F32)


def swap_halves(x):
    return pltpu.roll(x, HALF, 1)


def low_lanes(rows):
    return lax.broadcasted_iota(jnp.int32, (rows, LANES), 1) < HALF


def turn(index, by):
    return lax.rem(index + by, SIDE)


def start_all(copies):
    for copy in copies:
        copy.start()
    return copies


def wait_all(copies):
    for copy in copies:
        copy.wait()


def add(*terms):
    total = terms[0].astype(F32)
    for term in terms[1:]:
        total = total + term.astype(F32)
    return total.astype(BF16)


def cut_for_column(grad, target, sems, y, x, by, split):
    to_x = turn(x, by)
    copies = [
        pltpu.make_async_copy(
            grad.at[k, to_x, :, pl.ds(0, split)], target.at[:, pl.ds(k * split, split)], sems.at[k]
        )
        for k in range(SIDE)
    ]
    rest = grad.shape[3] - split
    copies.append(
        pltpu.make_async_copy(
            grad.at[turn(y, 2), to_x, :, pl.ds(split, rest)], target.at[:, pl.ds(SIDE * split, rest)], sems.at[SIDE]
        )
    )
    return copies


def cut_for_row(grad, target, sem, y, by, split):
    rest = grad.shape[3] - split
    return [pltpu.make_async_copy(grad.at[turn(y, by), :, :, pl.ds(split, rest)], target, sem)]


def first_send_kernel(split, here, grad, a1, b1, a3, b3, a2, column_sems, row_sems):
    y, x = here[0], here[1]
    copies = []
    for k, (by, target) in enumerate(((1, a1), (3, a3), (2, a2))):
        copies += cut_for_column(grad, target, column_sems.at[k], y, x, by, split)
    for k, (by, target) in enumerate(((1, b1), (3, b3))):
        copies += cut_for_row(grad, target, row_sems.at[k], y, by, split)
    wait_all(start_all(copies))


def fetch(source, target, sems):
    return start_all(
        [
            pltpu.make_async_copy(source.at[slot], target.at[slot], sems.at[slot])
            for slot in range(source.shape[0])
        ]
    )


def second_send_kernel(
    split, here, grad, a1, b1, a3, b3, a2, p0, p1, p2, p3, q0, q1, q2, q3, own_a, own_b, column_sems, row_sems
):
    y, x = here[0], here[1]
    column = start_all(cut_for_column(grad, own_a, column_sems, y, x, 0, split))
    row = start_all(cut_for_row(grad, own_b, row_sems.at[0], y, 0, split))
    wait_all(column)
    for by, out in enumerate((p0, p1, p2, p3)):
        lanes = pl.ds(pl.multiple_of(turn(y, by) * split, split), split)
        out[:, :split] = add(own_a[:, lanes], a1[:, lanes], a3[:, lanes], a2[:, lanes])
    p2[:, split:] = add(*(ref[:, SIDE * split :] for ref in (own_a, a1, a3, a2)))
    wait_all(row)
    for by, out in enumerate((q0, q1, q2, q3)):
        to_x = turn(x, by)
        out[...] = add(own_b[to_x], b1[to_x], b3[to_x])


def outgoing_kernel(holder, p0, p1, p3, p2, q0, q1, q3, q2, out, flat):
    order = out.shape[2]
    first_blocks = p0.shape[1] // order
    for block in range(flat.shape[0]):
        lanes = slice(block * order, (block + 1) * order)
        if block < first_blocks:
            flat[block] = add(p0[:, lanes], p1[:, lanes], p2[:, lanes], p3[:, lanes])
        else:
            rest = slice((block - first_blocks) * order, (block - first_blocks + 1) * order)
            flat[block] = add(q0[:, rest], q1[:, rest], q2[:, rest], q3[:, rest], p2[:, lanes])
    for slot in range(out.shape[0]):
        out[slot] = flat[holder[slot]]


def moment_right_kernel(moment_hbm, second_hbm, basis_hbm, packed, moment, second, basis, small_sems, sems):
    small = start_all(
        [
            pltpu.make_async_copy(moment_hbm, moment, small_sems.at[0]),
            pltpu.make_async_copy(second_hbm, second, small_sems.at[1]),
        ]
    )
    arrivals = fetch(basis_hbm, basis, sems)
    wait_all(small)
    low = low_lanes(HALF)
    for slot in range(moment.shape[0]):
        arrivals[slot].wait()
        turned = dot(moment[slot], basis[slot], NN)
        for pair in range(packed.shape[0] // 2):
            lanes = slice(pair * LANES, (pair + 1) * LANES)
            a = turned[:, lanes]
            b = second[slot, :, lanes].astype(F32)
            packed[2 * pair, slot] = jnp.where(low, a, swap_halves(b)).astype(BF16)
            packed[2 * pair + 1, slot] = jnp.where(low, swap_halves(a), b).astype(BF16)


def moment_left_kernel(packed, basis_hbm, out, basis, sems):
    arrivals = fetch(basis_hbm, basis, sems)
    order = basis.shape[1]
    for slot in range(out.shape[0]):
        both = packed[:, slot].reshape(order, LANES)
        out[slot, HALF:] = both.astype(F32).T[HALF:]
        arrivals[slot].wait()
        out[slot, :HALF] = dot(both[:, :HALF], basis[slot], TN)


def rotate_right_kernel(used, rows, moment_hbm, basis_hbm, first_hbm, packed, moment, first, basis, small_sems, sems):
    small = pltpu.make_async_copy(moment_hbm, moment, small_sems.at[0])
    arrivals = fetch(basis_hbm, basis, sems)
    small.start()
    small.wait()
    half = HALF // 2
    low = low_lanes(half)
    for slot in range(rows.shape[0]):
        grad = rows[slot]
        mixed = BETA_FIRST * moment[slot].astype(F32) + (1.0 - BETA_FIRST) * grad.astype(F32)
        first[slot] = jnp.where(used[slot] > 0, mixed, 0.0).astype(BF16)
    done = pltpu.make_async_copy(first, first_hbm, small_sems.at[1])
    done.start()
    for slot in range(rows.shape[0]):
        arrivals[slot].wait()
        turned = dot(rows[slot], basis[slot], NN)
        for pair in range(packed.shape[0] // 2):
            lanes = slice(pair * LANES, (pair + 1) * LANES)
            a = turned[:half, lanes]
            b = turned[half:, lanes]
            packed[2 * pair, slot] = jnp.where(low, a, swap_halves(b)).astype(BF16)
            packed[2 * pair + 1, slot] = jnp.where(low, swap_halves(a), b).astype(BF16)
    done.wait()


def rotate_left_kernel(packed, basis_hbm, ready, out, basis, sems):
    arrivals = fetch(basis_hbm, basis, sems)
    order = basis.shape[1]
    parts, half = packed.shape[0], packed.shape[2]
    for slot in range(out.shape[1]):
        both = packed[:, slot].reshape(parts * half, LANES)
        arrivals[slot].wait()
        cut = basis[slot].reshape(parts, 2, half, order)
        rot_grad = dot(both[:, :HALF], cut[:, 0].reshape(parts * half, order), TN) + dot(
            both[:, HALF:], cut[:, 1].reshape(parts * half, order), TN
        )
        rot_mom = BETA_FIRST * ready[slot, :HALF] + (1.0 - BETA_FIRST) * rot_grad
        variance = BETA_SECOND * ready[slot, HALF:] + (1.0 - BETA_SECOND) * rot_grad * rot_grad
        direction = (rot_mom / (jnp.sqrt(variance) + EPSILON)).astype(BF16)
        step = dot(direction, basis[slot], NT)
        joined = jnp.concatenate([step, variance], axis=0).T.astype(BF16)
        out[:, slot] = joined.reshape(parts, HALF, LANES)


def step_kernel(used, packed, basis_hbm, second_hbm, step, basis, second, sems, out_sems):
    arrivals = fetch(basis_hbm, basis, sems)
    low = low_lanes(HALF)
    done = []
    for slot in range(second.shape[0]):
        lefts = []
        for pair in range(packed.shape[0] // 2):
            lanes = slice(pair * LANES, (pair + 1) * LANES)
            a = packed[2 * pair, slot].astype(F32)
            b = packed[2 * pair + 1, slot].astype(F32)
            lefts.append(jnp.where(low, a, swap_halves(b)).astype(BF16))
            v = jnp.where(low, swap_halves(a), b)
            second[slot, :, lanes] = jnp.where(used[slot] > 0, v, 0.0).astype(BF16)
        done.append(pltpu.make_async_copy(second.at[slot], second_hbm.at[slot], out_sems.at[slot]))
        done[slot].start()
        arrivals[slot].wait()
        moved = dot(jnp.concatenate(lefts, axis=1), basis[slot], NT)
        step[:, slot] = moved.reshape(step.shape[0], step.shape[2], step.shape[3]).astype(BF16)
    wait_all(done)


def gram_tiles_kernel(
    here, rows, y2, x2, y1, y3, x1,
    own, left0, left1, left2, left3, right0, right1, right2, right3,
    across, down, grams, sems,
):
    y, x = here[0], here[1]
    slots, slab, order = rows.shape
    lines = SIDE * slab
    start = pl.multiple_of(y * lines, lines)
    arrivals = []
    for slot in range(slots):
        copies = []
        for back, ref in enumerate((rows, y1, y2, y3)):
            copies.append(pltpu.make_async_copy(ref.at[slot], down.at[back, slot], sems.at[slot, back]))
        for back, ref in enumerate((x1, x2)):
            copies.append(pltpu.make_async_copy(ref.at[slot], across.at[back, slot], sems.at[slot, SIDE + back]))
        arrivals.append(start_all(copies))
    for slot in range(slots):
        wait_all(arrivals[slot])
        panel = down[:, slot].reshape(lines, order)
        tile = dot(panel, across[:, slot].reshape(2 * slab, order), NT)
        own[slot] = dot(down[0, slot], panel, NT)
        for back, out in enumerate((left0, left1, left2, left3)):
            out[slot] = tile[back * slab : (back + 1) * slab].astype(out.dtype)
        columns = down[:, slot, :, pl.ds(start, lines)].reshape(lines, lines)
        grams[...] = dot(columns, panel, TN).reshape(grams.shape)
        for by, out in enumerate((right0, right1, right2, right3)):
            out[slot, :, :order] = grams[turn(x, by)].astype(out.dtype)
        right3[slot, :, order:] = dot(across[0, slot], panel, NT).astype(BF16)


def spread(pair, which):
    other = swap_halves(pair)
    low = low_lanes(pair.shape[0])
    twice = jnp.where(low, pair, other) if which == 0 else jnp.where(low, other, pair)
    return jnp.concatenate([twice, twice], axis=1)


def gram_sum_kernel(
    here, used, own, left0, left1, left2, left3, right0, right1, right2, right3, left_hbm, right_hbm,
    new_left_hbm, new_right_hbm, left, right, sems, out_sems,
):
    y, x = here[0], here[1]
    slots, slab, order = left.shape
    old = [
        start_all(
            [
                pltpu.make_async_copy(right_hbm.at[slot], right.at[slot], sems.at[slot, 0]),
                pltpu.make_async_copy(left_hbm.at[slot], left.at[slot], sems.at[slot, 1]),
            ]
        )
        for slot in range(slots)
    ]
    done = []
    lines = own.shape[2]
    column = lax.broadcasted_iota(jnp.int32, (slab, lines), 1) // HALF
    for slot in range(slots):
        is_used = used[slot] > 0
        wait_all(old[slot])
        for ahead, tile in enumerate((left0, left1, left2, left3)):
            back = (SIDE - ahead) % SIDE
            same = spread(own[slot, :, back // 2 * LANES :][:, :LANES], back % 2)
            first = order + back // 2 * LANES
            ahead_x = spread(right3[slot, :, first : first + LANES].astype(F32), back % 2)
            tile = tile[slot].astype(F32)
            gram = jnp.where(column == turn(x, 1), ahead_x, same)
            gram = jnp.where(column == turn(x, 3), spread(tile, 0), gram)
            gram = jnp.where(column == turn(x, 2), spread(tile, 1), gram)
            lanes = pl.ds(pl.multiple_of(turn(y, ahead) * lines, lines), lines)
            left[slot, :, lanes] = jnp.where(
                is_used, BETA_FACTOR * left[slot, :, lanes] + (1.0 - BETA_FACTOR) * gram, 0.0
            )
        gram = right0[slot]
        for term in (right1, right2, right3):
            gram = gram + term[slot, :, :order].astype(F32)
        right[slot] = jnp.where(is_used, BETA_FACTOR * right[slot] + (1.0 - BETA_FACTOR) * gram, 0.0)
        done += start_all(
            [
                pltpu.make_async_copy(right.at[slot], new_right_hbm.at[slot], out_sems.at[slot, 0]),
                pltpu.make_async_copy(left.at[slot], new_left_hbm.at[slot], out_sems.at[slot, 1]),
            ]
        )
    wait_all(done)


def along_x(value, by):
    pairs = [
        (y * SIDE + x, y * SIDE + (x + by) % SIDE) for y in range(SIDE) for x in range(SIDE)
    ]
    return lax.ppermute(value, "dp", pairs)


def along_y(value, by):
    pairs = [
        (y * SIDE + x, ((y + by) % SIDE) * SIDE + x) for y in range(SIDE) for x in range(SIDE)
    ]
    return lax.ppermute(value, "dp", pairs)


def call(kernel, name, ins, outs, scratch, products, moved):
    arrays = [pltpu.with_memory_space_constraint(array, space) if space == HBM else array for array, space in ins]
    return pl.pallas_call(
        kernel,
        in_specs=[pl.BlockSpec(memory_space=space) for _, space in ins],
        out_specs=[pl.BlockSpec(memory_space=space or VMEM) for _, _, space in outs],
        out_shape=[
            space(shape, dtype) if space == VMEM else jax.ShapeDtypeStruct(shape, dtype) for shape, dtype, space in outs
        ],
        scratch_shapes=scratch,
        compiler_params=pltpu.CompilerParams(vmem_limit_bytes=VMEM_BYTES),
        cost_estimate=pl.CostEstimate(flops=products * 2**27, bytes_accessed=moved * 2**20, transcendentals=0),
        name=name,
    )(*arrays)


def sum_replicas(grad, here, holder, slot_total, order, beside, between):
    rows, width = grad.shape[1], grad.shape[2]
    split = width // order // 6 * order
    rest = width - split
    grad = grad.reshape(SIDE, SIDE, rows, width)
    column, row = (rows, SIDE * split + rest), (SIDE, rows, rest)
    sent = call(
        functools.partial(first_send_kernel, split), "first_send", [(here, SMEM), (grad, HBM)],
        [(shape, BF16, VMEM) for shape in (column, row, column, row, column)],
        [pltpu.SemaphoreType.DMA((3, SIDE + 1)), pltpu.SemaphoreType.DMA((2,))], 0, 5,
    )
    got = [along_x(sent[0], 1), along_y(sent[1], 1), along_x(sent[2], 3), along_y(sent[3], 3), along_x(sent[4], 2)]
    got, early = lax.optimization_barrier((got, beside()))
    early = between(early)
    piece, piece_rest, both = (rows, split), (rows, rest), (rows, width)
    pieces = call(
        functools.partial(second_send_kernel, split), "second_send",
        [(here, SMEM), (grad, HBM)] + [(value, VMEM) for value in got],
        [(piece, BF16, None), (piece, BF16, VMEM), (both, BF16, VMEM), (piece, BF16, VMEM), (piece_rest, BF16, None)]
        + [(piece_rest, BF16, VMEM)] * 3,
        [
            pltpu.VMEM(column, BF16), pltpu.VMEM(row, BF16), pltpu.SemaphoreType.DMA((SIDE + 1,)),
            pltpu.SemaphoreType.DMA((1,)),
        ],
        0, 4,
    )
    p, q = [pieces[0]], [pieces[4]]
    for by in (1, 3, 2):
        p.append(along_y(pieces[by], by))
        q.append(along_x(pieces[4 + by], by))
    p, q, early = lax.optimization_barrier((p, q, early))
    outgoing = call(
        outgoing_kernel, "outgoing", [(holder, SMEM)] + [(value, VMEM) for value in p + q],
        [((slot_total, rows, order), BF16, VMEM)], [pltpu.VMEM((width // order, rows, order), BF16)], 0, 1,
    )[0]
    return outgoing, early


def on_device(
    grad_part,
    block_slot,
    left_factor,
    right_factor,
    first_moment,
    second_moment,
    left_basis,
    right_basis,
):
    owners = lax.axis_size("owner")
    replicas = lax.axis_size("dp")
    mine_dp = lax.axis_index("dp").astype(jnp.int32)
    mine_owner = lax.axis_index("owner")
    slots, slab, order = left_factor.shape
    part_rows = grad_part.shape[2]
    width = grad_part.shape[3]
    blocks = width // order

    slot_ids = jnp.arange(owners * slots, dtype=jnp.int32)
    matches = block_slot[None, :] == slot_ids[:, None]
    filled = jnp.any(matches, axis=1).astype(jnp.int32)
    holder = jnp.sum(jnp.where(matches, jnp.arange(blocks, dtype=jnp.int32)[None, :], 0), axis=1)
    used = lax.dynamic_slice_in_dim(filled, mine_owner * slots, slots)
    here = jnp.stack([mine_dp // SIDE, mine_dp % SIDE])

    slabs = (slots, slab, order)

    def exchange(value, axis):
        return lax.all_to_all(value, axis, split_axis=0, concat_axis=0, tiled=True)

    basis_scratch = [pltpu.VMEM((slots, order, order), BF16), pltpu.SemaphoreType.DMA((slots,))]
    chunks = (replicas, slots, slab, LANES)

    def moment_right():
        return call(
            moment_right_kernel, "moment_right",
            [(first_moment, HBM), (second_moment, HBM), (right_basis, HBM)], [(chunks, BF16, VMEM)],
            [pltpu.VMEM(slabs, BF16), pltpu.VMEM(slabs, BF16), basis_scratch[0], pltpu.SemaphoreType.DMA((2,)), basis_scratch[1]],
            3, 8,
        )[0]

    outgoing, early = sum_replicas(
        grad_part[0], here, holder, owners * slots, order, moment_right, lambda value: exchange(value, "dp")
    )
    incoming = exchange(outgoing.reshape(owners, slots, part_rows, order), "owner")
    ready = call(
        moment_left_kernel, "moment_left", [(early, VMEM), (left_basis, HBM)],
        [((slots, 2 * slab, order), F32, VMEM)], basis_scratch, 3, 8,
    )[0]
    incoming, ready = lax.optimization_barrier((incoming, ready))
    rows = incoming.transpose(1, 0, 2, 3).reshape(slabs)

    new_first, packed = call(
        rotate_right_kernel, "rotate_right",
        [(used, SMEM), (rows, VMEM), (first_moment, HBM), (right_basis, HBM)],
        [(slabs, BF16, HBM), ((replicas, slots, slab // 2, LANES), BF16, VMEM)],
        [pltpu.VMEM(slabs, BF16), pltpu.VMEM(slabs, BF16), basis_scratch[0], pltpu.SemaphoreType.DMA((2,)), basis_scratch[1]],
        3, 8,
    )
    rows, packed = lax.optimization_barrier((rows, packed))
    packed = exchange(packed, "dp")
    near = [along_y(rows, 2), along_x(rows, 2), along_y(rows, 1), along_y(rows, 3), along_x(rows, 1)]
    turned = call(
        rotate_left_kernel, "rotate_left", [(packed, VMEM), (left_basis, HBM), (ready, VMEM)],
        [(chunks, BF16, VMEM)], basis_scratch, 9, 8,
    )[0]
    near, turned = lax.optimization_barrier((near, turned))
    turned = exchange(turned, "dp")
    tiles = call(
        gram_tiles_kernel, "gram_tiles", [(here, SMEM)] + [(value, HBM) for value in [rows] + near],
        [((slots, slab, SIDE * slab), F32, VMEM)]
        + [((slots, slab, 2 * slab), F32 if k == 0 else BF16, VMEM) for k in range(SIDE)]
        + [(slabs, F32, VMEM), (slabs, BF16, VMEM), (slabs, BF16, VMEM), ((slots, slab, order + SIDE * slab), BF16, VMEM)],
        [
            pltpu.VMEM((2, slots, slab, order), BF16), pltpu.VMEM((SIDE, slots, slab, order), BF16),
            pltpu.VMEM((SIDE, slab, order), F32), pltpu.SemaphoreType.DMA((slots, SIDE + 2)),
        ],
        9, 6,
    )
    lefts = [tiles[1]] + [along_y(tiles[1 + back], SIDE - back) for back in (1, 2, 3)]
    rights = [tiles[1 + SIDE]] + [along_x(tiles[1 + SIDE + by], by) for by in (1, 2, 3)]
    early_lefts, turned = lax.optimization_barrier((lefts[1:2], turned))
    lefts = [lefts[0], *early_lefts, *lefts[2:]]
    new_second, step = call(
        step_kernel, "step_rows", [(used, SMEM), (turned, VMEM), (right_basis, HBM)],
        [(slabs, BF16, HBM), ((owners, slots, part_rows, order), BF16, VMEM)],
        [basis_scratch[0], pltpu.VMEM(slabs, BF16), basis_scratch[1], pltpu.SemaphoreType.DMA((slots,))], 3, 8,
    )
    returned = exchange(step, "owner")
    rights, step = lax.optimization_barrier((rights, step))
    new_left, new_right = call(
        gram_sum_kernel, "gram_sum",
        [(here, SMEM), (used, SMEM)] + [(value, VMEM) for value in [tiles[0]] + lefts + rights]
        + [(left_factor, HBM), (right_factor, HBM)],
        [(slabs, F32, HBM)] * 2,
        [
            pltpu.VMEM(slabs, F32), pltpu.VMEM(slabs, F32), pltpu.SemaphoreType.DMA((slots, 2)),
            pltpu.SemaphoreType.DMA((slots, 2)),
        ],
        0, 8,
    )

    picked = returned.reshape(owners * slots, part_rows, order).at[block_slot].get(mode="promise_in_bounds")
    update = picked.transpose(1, 0, 2).reshape(part_rows, width)
    return new_left, new_right, new_first, new_second, update


def solution(mesh):
    slabs = P("owner", "dp", None)
    whole_slots = P("owner", None, None)
    return jax.shard_map(
        on_device,
        mesh=mesh,
        in_specs=(
            P("dp", None, "owner", None),
            P(),
            slabs,
            slabs,
            slabs,
            slabs,
            whole_slots,
            whole_slots,
        ),
        out_specs=(slabs, slabs, slabs, slabs, P(("dp", "owner"), None)),
        check_vma=False,
    )
```
